32 devices in a mesh: parts: 2 (over x), row: 8 (over z, y), col: 2 (over core).
Axes of the slice: x: 2, y: 2, z: 4, core: 2. Of those that a mesh axis runs over, the one named last changes fastest.
Arguments:
- spectra: bfloat16 [4, 32, 2, 32, 1024], P('parts', None, None, ('row', 'col')), parts along dimension 0, may hold values from -6 to 6
- window_flags: int32 [64, 32], P('parts', ('row', 'col')), parts along dimension 0, may hold values 0 or 1
Outputs:
- cross: float32 [4, 2, 2, 16, 32, 1024], P('parts', None, 'col', None, 'row'), parts along dimension 0
The draws below stay inside these ranges and needn't reach their ends.
There are 2 independent parts, one for each index of `parts`. The reference program is written for one: setup_inputs(seed, part) draws one part's arguments, and reference() takes and returns one part's arrays. A program takes and returns all parts, laid end to end along the dimension named above; each array names one. Nothing has to cross between parts.
All inputs are finite; a program needn't handle non-finite values. No bound on the sum of `window_flags` on one device may be relied on, other than what follows from the above.
Results may differ from the reference program's by a relative error of at most 0.0034.
Values may be sent and summed in bfloat16 or wider, within the bound.
No kernel may reach another device: no remote copies, remote signals or barrier semaphores. Data moves between devices by JAX's collectives and lax.ppermute only.
A program may use at most 256 MiB of HBM per device.

```python
import jax
import jax.numpy as jnp

CH_DEV = 2
W = 32
BANDS = 2
FB = 1024
HALFWIN = 64
C = 32
N_ROW = 8
N_COL = 2


def plant(entries, stream_key, least, largest):
    extent = entries.shape
    spot = [jax.random.randint(jax.random.fold_in(stream_key, axis), (), 0, extent[axis]) for axis in range(len(extent))]
    entries = entries.at[tuple(spot)].set(least)
    longest = extent.index(max(extent))
    spot[longest] = (spot[longest] + 1) % extent[longest]
    return entries.at[tuple(spot)].set(largest)


def block_levels(own_key, shape, cuts, least, top_value):
    gain, own = 1.0, jax.random.fold_in(own_key, 6)
    for axis_at, blocks in cuts:
        draws = jnp.exp(jax.random.uniform(jax.random.fold_in(own, axis_at), (blocks,), jnp.float32, least / len(cuts), top_value / len(cuts)))
        gain = gain * jnp.repeat(draws, shape[axis_at] // blocks).reshape([-1 if axis == axis_at else 1 for axis in range(len(shape))])
    return gain


def centred(key, extent, spread, bound, pieces=(), kind=jnp.bfloat16):
    drawn = jax.random.normal(key, extent, jnp.float32) * spread
    if len(pieces) > 0:
        drawn = block_levels(key, extent, pieces, -0.22, 0.18) * drawn
    return jnp.clip(drawn, min=-bound, max=bound).astype(kind)


def setup_inputs(seed: int = 0, part: int = 0) -> dict:
    key_of = jax.random.split(jax.random.key(seed), 3)
    own_keys = jax.random.split(jax.random.fold_in(key_of[2], part), 3)
    return {
        "spectra": centred(own_keys[0], (BANDS, W, 2, C, FB), 1.0, 6.0, ((3, 16),)),
        "window_flags": plant((jax.random.randint(own_keys[1], (W, C), 0, 4) < 3).astype(jnp.int32), jax.random.fold_in(own_keys[1], 1), 0, 1),
    }


epsilon = 1e-06

def window_mean(magnitude):
    bins = magnitude.shape[-1]
    lead = [(0, 0)] * (magnitude.ndim - 1)
    padded = jnp.pad(magnitude, lead + [(HALFWIN + 1, HALFWIN)])
    running = jnp.cumsum(padded, axis=-1)
    total = running[..., 2 * HALFWIN + 1:] - running[..., :bins]
    positions = jnp.arange(bins, dtype=jnp.int32)
    counted = (jnp.minimum(positions + HALFWIN, bins - 1) - jnp.maximum(positions - HALFWIN, 0) + 1).astype(jnp.float32)
    return total / counted

def whiten(values):
    magnitude = jnp.sqrt(values[:, :, 0] * values[:, :, 0] + values[:, :, 1] * values[:, :, 1])
    smooth = window_mean(magnitude)
    return (values / (smooth[:, :, None] + epsilon)).astype(jnp.bfloat16)

def reference(spectra, window_flags):
    flagged = spectra.astype(jnp.float32) * window_flags.astype(jnp.float32)[None, :, None, :, None]
    whitened = whiten(flagged)
    grouped = whitened.reshape(BANDS, W, 2, N_ROW, N_COL, CH_DEV, FB)
    total = N_ROW * N_COL * CH_DEV
    half_size = total // N_COL
    second = jnp.arange(total, dtype=jnp.int32)
    results = []
    for band_index in range(BANDS):
        halves = []
        for half_index in range(N_COL):
            first_rows = grouped[band_index, :, :, :, half_index].reshape(W, 2, half_size, FB).astype(jnp.float32)
            all_rows = whitened[band_index].astype(jnp.float32)
            prods = jnp.einsum('wpif,wqjf->pqijf', first_rows, all_rows)
            real_part = prods[0, 0] + prods[1, 1]
            imag_part = prods[1, 0] - prods[0, 1]
            slot = jnp.arange(half_size, dtype=jnp.int32)
            first = (slot // CH_DEV * N_COL + half_index) * CH_DEV + slot % CH_DEV
            keep = (first[:, None] <= second[None, :]).astype(jnp.float32)[:, :, None]
            halves.append(jnp.stack([real_part * keep, imag_part * keep], axis=0))
        results.append(jnp.stack(halves, axis=1))
    return jnp.stack(results, axis=0)
```

```python
import functools

import jax
import jax.numpy as jnp
from jax import lax
from jax.experimental import pallas as pl
from jax.experimental.pallas import tpu as pltpu
from jax.sharding import PartitionSpec as P

HALFWIN = 64
LANES = 128
SUB = 8

epsilon = 1e-06


def window_mean(magnitude):
    bins = magnitude.shape[-1]
    lead = [(0, 0)] * (magnitude.ndim - 1)
    padded = jnp.pad(magnitude, lead + [(HALFWIN + 1, HALFWIN)])
    running = jnp.cumsum(padded, axis=-1)
    total = running[..., 2 * HALFWIN + 1 :] - running[..., :bins]
    positions = jnp.arange(bins, dtype=jnp.int32)
    counted = (
        jnp.minimum(positions + HALFWIN, bins - 1) - jnp.maximum(positions - HALFWIN, 0) + 1
    ).astype(jnp.float32)
    return total / counted


def whiten_plain(spectra, window_flags, devices):
    bands, windows, parts, chans, bins = spectra.shape
    flags = window_flags.astype(jnp.float32)[None, :, None, :, None]
    values = spectra.astype(jnp.float32) * flags
    magnitude = jnp.sqrt(values[:, :, 0] * values[:, :, 0] + values[:, :, 1] * values[:, :, 1])
    smooth = window_mean(magnitude)
    white = (values / (smooth[:, :, None] + epsilon)).astype(jnp.bfloat16)
    own = bands * bins // devices
    white = white.reshape(bands, windows, parts, chans, bins // own, own)
    white = white.transpose(0, 4, 3, 2, 1, 5)
    return white.reshape(devices, chans * parts * windows, own)


def cross_plain(got, rows, cols, chans, windows):
    own = got.shape[-1]
    data = got.reshape(rows * cols * chans, 2, windows, own)
    prods = jnp.einsum("apwf,jqwf->pqajf", data, data, preferred_element_type=jnp.float32)
    both = jnp.stack([prods[0, 0] + prods[1, 1], prods[1, 0] - prods[0, 1]])
    both = both.reshape(2, rows, cols, chans, rows, cols * chans, own)
    both = both.transpose(4, 2, 0, 1, 3, 5, 6).astype(jnp.bfloat16)
    return both.reshape(rows * cols, 2 * rows * chans * cols * chans, own)


def finish_plain(got, bands, bins, rows, cols, chans):
    own = got.shape[-1]
    row, col = lax.axis_index("row"), lax.axis_index("col")
    data = got.reshape(bands, bins // own, 2, rows * chans, cols * chans, own)
    data = data.transpose(0, 2, 3, 4, 1, 5).reshape(
        bands, 2, rows * chans, cols * chans, bins
    )
    slot = jnp.arange(rows * chans, dtype=jnp.int32)
    first = (slot // chans * cols + col) * chans + slot % chans
    second = row * cols * chans + jnp.arange(cols * chans, dtype=jnp.int32)
    keep = (first[:, None] <= second[None, :])[:, :, None]
    return jnp.where(keep, data.astype(jnp.float32), 0.0)[:, :, None]


def whiten_kernel(flags_ref, x_ref, out_ref, white_ref, *, chans):
    bands, windows, _, group, _ = x_ref.shape
    chunks = group // chans
    step = 8
    rows = step * group
    row_id = lax.broadcasted_iota(jnp.int32, (rows, LANES), 0) % group
    lane_id = lax.broadcasted_iota(jnp.int32, (rows, LANES), 1)
    spot = row_id // chans * LANES + lane_id
    last = chunks * LANES - 1
    counted = jnp.minimum(spot + HALFWIN, last) - jnp.maximum(spot - HALFWIN, 0) + 1
    inv_count = 1.0 / counted.astype(jnp.float32)
    has_prev = row_id >= chans
    has_next = row_id < group - chans
    k_id = lax.broadcasted_iota(jnp.int32, (group, LANES), 0) % chans
    src = lax.broadcasted_iota(jnp.int32, (LANES, 3 * LANES), 0)
    dst = lax.broadcasted_iota(jnp.int32, (LANES, 3 * LANES), 1) - LANES
    band_mat = jnp.where(jnp.abs(src - dst) <= HALFWIN, 1.0, 0.0).astype(jnp.bfloat16)

    def body(n, carry):
        b = n // (windows // step)
        w0 = n % (windows // step) * step
        x = x_ref[b, pl.ds(w0, step)].astype(jnp.float32)
        keeps = []
        for s in range(step):
            keep = jnp.full((group, LANES), flags_ref[0, w0 + s], jnp.int32)
            for k in range(1, chans):
                keep = jnp.where(k_id == k, flags_ref[k, w0 + s], keep)
            keeps.append(keep)
        keep = jnp.stack(keeps).astype(jnp.float32)
        re = (x[:, 0] * keep).reshape(rows, LANES)
        im = (x[:, 1] * keep).reshape(rows, LANES)
        mag = jnp.sqrt(re * re + im * im)
        high = mag.astype(jnp.bfloat16)
        low = (mag - high.astype(jnp.float32)).astype(jnp.bfloat16)
        sums = jnp.dot(high, band_mat, preferred_element_type=jnp.float32) + jnp.dot(
            low, band_mat, preferred_element_type=jnp.float32
        )
        total = sums[:, LANES : 2 * LANES]
        total += jnp.where(has_prev, pltpu.roll(sums[:, 2 * LANES :], chans, 0), 0.0)
        total += jnp.where(has_next, pltpu.roll(sums[:, :LANES], rows - chans, 0), 0.0)
        inv = 1.0 / (total * inv_count + epsilon)
        for p, part in enumerate((re, im)):
            start = pl.multiple_of(((b * 2 + p) * windows + w0) * group, rows)
            white_ref[pl.ds(start, rows), :] = part * inv
        return carry

    lax.fori_loop(0, bands * windows // step, body, 0)
    for b in range(bands):
        for c in range(chunks):
            for k in range(chans):
                for p in range(2):
                    start = (b * 2 + p) * windows * group + c * chans + k
                    slab = white_ref[pl.ds(start, windows, stride=group), :]
                    at = (k * 2 + p) * windows
                    out_ref[b * chunks + c, at : at + windows, :] = slab.astype(jnp.bfloat16)


def whiten_packed(spectra, window_flags):
    bands, windows, parts, chans, bins = spectra.shape
    chunks = bins // LANES
    view = spectra.reshape(bands, windows, parts, chans, chunks, LANES)
    view = view.transpose(0, 1, 2, 4, 3, 5).reshape(bands, windows, parts, chunks * chans, LANES)
    flags = window_flags.T
    rows = chans * parts * windows
    return pl.pallas_call(
        functools.partial(whiten_kernel, chans=chans),
        out_shape=jax.ShapeDtypeStruct((bands * chunks, rows, LANES), jnp.bfloat16),
        in_specs=[
            pl.BlockSpec(memory_space=pltpu.SMEM),
            pl.BlockSpec(memory_space=pltpu.VMEM),
        ],
        out_specs=pl.BlockSpec(memory_space=pltpu.VMEM),
        scratch_shapes=[
            pltpu.VMEM((bands * parts * windows * chunks * chans, LANES), jnp.float32)
        ],
        compiler_params=pltpu.CompilerParams(vmem_limit_bytes=32 * 2**20),
        name="whiten",
    )(flags, view)


def cross_kernel(x_ref, out_ref, flat_ref, data_ref, *, rows, cols, chans, windows):
    channels = rows * cols * chans
    own_rows = 2 * windows
    per_row = cols * chans
    for s in range(rows * cols):
        flat_ref[s * chans * own_rows : (s + 1) * chans * own_rows, :] = x_ref[s].astype(
            jnp.float32
        )

    def spread(w, carry):
        for jb in range(channels // SUB):
            at = pl.ds(jb * SUB, SUB)
            re = flat_ref[pl.ds(jb * SUB * own_rows + w, SUB, stride=own_rows), :]
            im = flat_ref[pl.ds(jb * SUB * own_rows + windows + w, SUB, stride=own_rows), :]
            data_ref[0, w, at, :] = re
            data_ref[1, w, at, :] = im
            data_ref[2, w, at, :] = re + im
            data_ref[3, w, at, :] = im - re
        return carry

    lax.fori_loop(0, windows, spread, 0)

    low = lax.broadcasted_iota(jnp.int32, (SUB, LANES), 0) < per_row
    for r_first in range(rows):
        blocks = list(range(r_first * per_row // SUB, channels // SUB))
        groups = [blocks[max(0, i - 2) : i] for i in range(len(blocks), 0, -2)]
        for group in groups:

            def body(w, sums, group=group, r_first=r_first):
                out = []
                js = [
                    [data_ref[t, w, pl.ds(jb * SUB, SUB), :] for t in (0, 3, 2)] for jb in group
                ]
                for a in range(per_row):
                    at = pl.ds(r_first * per_row + a, 1)
                    total, imag, real = (data_ref[t, w, at, :] for t in (2, 1, 0))
                    for n in range(len(group)):
                        s1, s2, s3 = sums[a * len(group) + n]
                        out.append(
                            (
                                s1 + js[n][0] * total,
                                s2 + js[n][1] * imag,
                                s3 + js[n][2] * real,
                            )
                        )
                return tuple(out)

            zero = jnp.zeros((SUB, LANES), jnp.float32)
            sums = lax.fori_loop(
                0, windows, body, ((zero, zero, zero),) * (per_row * len(group)), unroll=4
            )
            for n, jb in enumerate(group):
                for h in range(cols):
                    one = sums[(h * chans) * len(group) + n]
                    two = sums[(h * chans + 1) * len(group) + n]
                    for q in range(2):
                        va = one[0] - one[2] if q else one[0] + one[1]
                        vb = two[0] - two[2] if q else two[0] + two[1]
                        even = jnp.where(low, va, pltpu.roll(vb, per_row, 0))
                        odd = jnp.where(low, pltpu.roll(va, per_row, 0), vb)
                        at = (q * rows + r_first) * SUB
                        r = jb * SUB // per_row
                        out_ref[r * cols + h, at : at + SUB, :] = even.astype(jnp.bfloat16)
                        out_ref[(r + 1) * cols + h, at : at + SUB, :] = odd.astype(jnp.bfloat16)


def cross_packed(got, rows, cols, chans, windows):
    devices = rows * cols
    channels = devices * chans
    return pl.pallas_call(
        functools.partial(cross_kernel, rows=rows, cols=cols, chans=chans, windows=windows),
        out_shape=jax.ShapeDtypeStruct((devices, 2 * rows * SUB, LANES), jnp.bfloat16),
        in_specs=[pl.BlockSpec(memory_space=pltpu.VMEM)],
        out_specs=pl.BlockSpec(memory_space=pltpu.VMEM),
        scratch_shapes=[
            pltpu.VMEM((channels * 2 * windows, LANES), jnp.float32),
            pltpu.VMEM((4, windows, channels, LANES), jnp.float32),
        ],
        compiler_params=pltpu.CompilerParams(vmem_limit_bytes=32 * 2**20),
        name="cross",
    )(got)


def finish_kernel(x_ref, out_ref, *, rows, cols, chans):
    bands, _, _, _, pairs, _, _ = out_ref.shape
    row, col = lax.axis_index("row"), lax.axis_index("col")
    per_row = cols * chans
    sub = lax.broadcasted_iota(jnp.int32, (2, rows, SUB, LANES), 2)
    r_first = lax.broadcasted_iota(jnp.int32, (2, rows, SUB, LANES), 1)
    low = sub < per_row
    second = row * per_row + sub % per_row
    keep = [r_first * per_row + col * chans + k <= second for k in range(chans)]
    for b in range(bands):
        for c in range(pairs):
            s = (b * pairs + c) * 2
            one = x_ref[s].astype(jnp.float32).reshape(2, rows, SUB, LANES)
            two = x_ref[s + 1].astype(jnp.float32).reshape(2, rows, SUB, LANES)
            even = jnp.where(low, one, pltpu.roll(two, per_row, 2))
            odd = jnp.where(low, pltpu.roll(one, per_row, 2), two)
            out_ref[b, :, :, 0, c] = jnp.where(keep[0], even, 0.0)
            out_ref[b, :, :, 1, c] = jnp.where(keep[1], odd, 0.0)


def finish_packed(got, bands, bins, rows, cols, chans):
    chunks = bins // LANES
    out = pl.pallas_call(
        functools.partial(finish_kernel, rows=rows, cols=cols, chans=chans),
        out_shape=jax.ShapeDtypeStruct(
            (bands, 2, rows, chans, chunks // 2, SUB, LANES), jnp.float32
        ),
        in_specs=[pl.BlockSpec(memory_space=pltpu.VMEM)],
        out_specs=pl.BlockSpec(memory_space=pltpu.VMEM),
        compiler_params=pltpu.CompilerParams(vmem_limit_bytes=32 * 2**20),
        name="finish",
    )(got)
    out = out.reshape(bands, 2, rows * chans, chunks, cols * chans, LANES)
    out = out.transpose(0, 1, 2, 4, 3, 5)
    return out.reshape(bands, 2, 1, rows * chans, cols * chans, bins)


def on_device(spectra, window_flags):
    bands, windows, _, chans, bins = spectra.shape
    rows, cols = lax.axis_size("row"), lax.axis_size("col")
    devices = rows * cols
    packed = (
        bands * bins == devices * LANES
        and bins % (2 * LANES) == 0
        and chans == 2
        and cols * chans * 2 == SUB
        and windows % 16 == 0
    )
    if packed:
        payload = whiten_packed(spectra, window_flags)
    else:
        payload = whiten_plain(spectra, window_flags, devices)
    got = lax.all_to_all(payload, ("row", "col"), 0, 0, tiled=True)
    if packed:
        result = cross_packed(got, rows, cols, chans, windows)
    else:
        result = cross_plain(got, rows, cols, chans, windows)
    back = lax.all_to_all(result, ("row", "col"), 0, 0, tiled=True)
    if packed:
        return finish_packed(back, bands, bins, rows, cols, chans)
    return finish_plain(back, bands, bins, rows, cols, chans)


def solution(mesh):
    in_specs = (P("parts", None, None, ("row", "col"), None), P("parts", ("row", "col")))
    out_specs = P("parts", None, "col", None, "row", None)
    return jax.shard_map(
        on_device, mesh=mesh, in_specs=in_specs, out_specs=out_specs, check_vma=False
    )
```

```python
import functools

import jax
import jax.numpy as jnp
from jax import lax
from jax.experimental import pallas as pl
from jax.experimental.pallas import tpu as pltpu
from jax.sharding import PartitionSpec as P

HALFWIN = 64
LANES = 128
SUB = 8

epsilon = 1e-06


def window_mean(magnitude):
    bins = magnitude.shape[-1]
    lead = [(0, 0)] * (magnitude.ndim - 1)
    padded = jnp.pad(magnitude, lead + [(HALFWIN + 1, HALFWIN)])
    running = jnp.cumsum(padded, axis=-1)
    total = running[..., 2 * HALFWIN + 1 :] - running[..., :bins]
    positions = jnp.arange(bins, dtype=jnp.int32)
    counted = (
        jnp.minimum(positions + HALFWIN, bins - 1) - jnp.maximum(positions - HALFWIN, 0) + 1
    ).astype(jnp.float32)
    return total / counted


def whiten_plain(spectra, window_flags, devices):
    bands, windows, parts, chans, bins = spectra.shape
    flags = window_flags.astype(jnp.float32)[None, :, None, :, None]
    values = spectra.astype(jnp.float32) * flags
    magnitude = jnp.sqrt(values[:, :, 0] * values[:, :, 0] + values[:, :, 1] * values[:, :, 1])
    smooth = window_mean(magnitude)
    white = (values / (smooth[:, :, None] + epsilon)).astype(jnp.bfloat16)
    own = bands * bins // devices
    white = white.reshape(bands, windows, parts, chans, bins // own, own)
    white = white.transpose(0, 4, 3, 2, 1, 5)
    return white.reshape(devices, chans * parts * windows, own)


def cross_plain(got, rows, cols, chans, windows):
    own = got.shape[-1]
    data = got.reshape(rows * cols * chans, 2, windows, own)
    prods = jnp.einsum("apwf,jqwf->pqajf", data, data, preferred_element_type=jnp.float32)
    both = jnp.stack([prods[0, 0] + prods[1, 1], prods[1, 0] - prods[0, 1]])
    both = both.reshape(2, rows, cols, chans, rows, cols * chans, own)
    both = both.transpose(4, 2, 0, 1, 3, 5, 6).astype(jnp.bfloat16)
    return both.reshape(rows * cols, 2 * rows * chans * cols * chans, own)


def finish_plain(got, bands, bins, rows, cols, chans):
    own = got.shape[-1]
    row, col = lax.axis_index("row"), lax.axis_index("col")
    data = got.reshape(bands, bins // own, 2, rows * chans, cols * chans, own)
    data = data.transpose(0, 2, 3, 4, 1, 5).reshape(
        bands, 2, rows * chans, cols * chans, bins
    )
    slot = jnp.arange(rows * chans, dtype=jnp.int32)
    first = (slot // chans * cols + col) * chans + slot % chans
    second = row * cols * chans + jnp.arange(cols * chans, dtype=jnp.int32)
    keep = (first[:, None] <= second[None, :])[:, :, None]
    return jnp.where(keep, data.astype(jnp.float32), 0.0)[:, :, None]


def whiten_kernel(flags_ref, x_ref, *refs, chans, tiles):
    out_refs, white_ref = refs[:-1], refs[-1]
    bands, windows, _, group, _ = x_ref.shape
    chunks = group // chans
    step = 8
    rows = step * group
    row_id = lax.broadcasted_iota(jnp.int32, (rows, LANES), 0) % group
    lane_id = lax.broadcasted_iota(jnp.int32, (rows, LANES), 1)
    spot = row_id // chans * LANES + lane_id
    last = chunks * LANES - 1
    counted = jnp.minimum(spot + HALFWIN, last) - jnp.maximum(spot - HALFWIN, 0) + 1
    inv_count = 1.0 / counted.astype(jnp.float32)
    has_prev = row_id >= chans
    has_next = row_id < group - chans
    k_id = lax.broadcasted_iota(jnp.int32, (group, LANES), 0) % chans
    src = lax.broadcasted_iota(jnp.int32, (LANES, 3 * LANES), 0)
    dst = lax.broadcasted_iota(jnp.int32, (LANES, 3 * LANES), 1) - LANES
    band_mat = jnp.where(jnp.abs(src - dst) <= HALFWIN, 1.0, 0.0).astype(jnp.bfloat16)

    def body(n, carry):
        b = n // (windows // step)
        w0 = n % (windows // step) * step
        x = x_ref[b, pl.ds(w0, step)].astype(jnp.float32)
        keeps = []
        for s in range(step):
            keep = jnp.full((group, LANES), flags_ref[0, w0 + s], jnp.int32)
            for k in range(1, chans):
                keep = jnp.where(k_id == k, flags_ref[k, w0 + s], keep)
            keeps.append(keep)
        keep = jnp.stack(keeps).astype(jnp.float32)
        re = (x[:, 0] * keep).reshape(rows, LANES)
        im = (x[:, 1] * keep).reshape(rows, LANES)
        mag = jnp.sqrt(re * re + im * im)
        high = mag.astype(jnp.bfloat16)
        low = (mag - high.astype(jnp.float32)).astype(jnp.bfloat16)
        sums = jnp.dot(high, band_mat, preferred_element_type=jnp.float32) + jnp.dot(
            low, band_mat, preferred_element_type=jnp.float32
        )
        total = sums[:, LANES : 2 * LANES]
        total += jnp.where(has_prev, pltpu.roll(sums[:, 2 * LANES :], chans, 0), 0.0)
        total += jnp.where(has_next, pltpu.roll(sums[:, :LANES], rows - chans, 0), 0.0)
        inv = 1.0 / (total * inv_count + epsilon)
        for p, part in enumerate((re, im)):
            start = pl.multiple_of(((b * 2 + p) * windows + w0) * group, rows)
            white_ref[pl.ds(start, rows), :] = part * inv
        return carry

    lax.fori_loop(0, bands * windows // step, body, 0)
    row = lax.axis_index("row")
    for n, out_ref in enumerate(out_refs):
        for t in range(tiles):
            place = (row ^ n) * tiles + t
            b, c = place // chunks, place % chunks
            for k in range(chans):
                for p in range(2):
                    start = (b * 2 + p) * windows * group + c * chans + k
                    slab = white_ref[pl.ds(start, windows, stride=group), :]
                    at = (k * 2 + p) * windows
                    out_ref[t, at : at + windows, :] = slab.astype(jnp.bfloat16)


def whiten_packed(spectra, window_flags, rows):
    bands, windows, parts, chans, bins = spectra.shape
    chunks = bins // LANES
    tiles = bands * chunks // rows
    view = spectra.reshape(bands, windows, parts, chans, chunks, LANES)
    view = view.transpose(0, 1, 2, 4, 3, 5).reshape(bands, windows, parts, chunks * chans, LANES)
    piece = jax.ShapeDtypeStruct((tiles, chans * parts * windows, LANES), jnp.bfloat16)
    return pl.pallas_call(
        functools.partial(whiten_kernel, chans=chans, tiles=tiles),
        out_shape=[piece] * rows,
        in_specs=[
            pl.BlockSpec(memory_space=pltpu.SMEM),
            pl.BlockSpec(memory_space=pltpu.VMEM),
        ],
        out_specs=[pl.BlockSpec(memory_space=pltpu.VMEM)] * rows,
        scratch_shapes=[
            pltpu.VMEM((bands * parts * windows * chunks * chans, LANES), jnp.float32)
        ],
        compiler_params=pltpu.CompilerParams(vmem_limit_bytes=32 * 2**20),
        cost_estimate=pl.CostEstimate(flops=10**9, bytes_accessed=2**20, transcendentals=0),
        name="whiten",
    )(window_flags.T, view)


def cross_kernel(*refs, rows, chans, tiles, windows):
    got, other, out_refs = refs[:rows], refs[rows : 2 * rows], refs[2 * rows : 3 * rows]
    first_ref, second_ref = refs[3 * rows :]
    firsts = rows * chans
    row = lax.axis_index("row")

    for n in range(rows):
        for s, ref in enumerate((got[n], other[n])):
            for t in range(tiles):
                for k in range(chans):
                    at = k * 2 * windows
                    re = ref[t, at : at + windows, :].astype(jnp.float32)
                    im = ref[t, at + windows : at + 2 * windows, :].astype(jnp.float32)
                    both = re + im
                    second_ref[s, n, t, k, 0] = re
                    second_ref[s, n, t, k, 1] = im - re
                    second_ref[s, n, t, k, 2] = both
                    if s == 0:
                        slot = pl.ds((row ^ n) * chans + k, windows, stride=firsts)
                        first_ref[0, t, slot, :] = both
                        first_ref[1, t, slot, :] = im
                        first_ref[2, t, slot, :] = re

    half = rows // 2
    blocks = firsts // SUB
    zero = jnp.zeros((SUB, LANES), jnp.float32)
    top = row // half
    for m in range(half):
        for s in range(2):
            for t in range(tiles):
                n_up = m + (1 - top) * half
                n_low = m + top * half
                work = [(n_up, k, blocks) for k in range(chans)]
                work += [(n_low, k, blocks // 2) for k in range(chans)]

                def body(w, sums, work=work, s=s, t=t):
                    base = pl.multiple_of(w * firsts, firsts)
                    fs = [
                        [first_ref[q, t, pl.ds(base + i * SUB, SUB), :] for q in range(3)]
                        for i in range(blocks)
                    ]
                    out = []
                    at = 0
                    for n, k, count in work:
                        g = [second_ref[s, n, t, k, q, pl.ds(w, 1), :] for q in range(3)]
                        for i in range(count):
                            s1, s2, s3 = sums[at]
                            at += 1
                            out.append(
                                (s1 + g[0] * fs[i][0], s2 + g[1] * fs[i][1], s3 + g[2] * fs[i][2])
                            )
                    return tuple(out)

                total = sum(count for _, _, count in work)
                sums = lax.fori_loop(0, windows, body, ((zero, zero, zero),) * total, unroll=4)
                parts = []
                at = 0
                for _, k, count in work:
                    mine = sums[at : at + count]
                    at += count
                    for q in range(2):
                        vals = [x[0] - x[2] if q else x[0] + x[1] for x in mine]
                        vals += [zero] * (blocks - count)
                        parts.append(jnp.concatenate(vals).astype(jnp.bfloat16))

                def put(up_ref, low_ref, parts=parts, s=s, t=t):
                    for e, ref in enumerate((up_ref, low_ref)):
                        for k in range(chans):
                            for q in range(2):
                                spot = ((q * 2 + s) * chans + k) * firsts
                                ref[t, spot : spot + firsts, :] = parts[(e * chans + k) * 2 + q]

                pl.when(top == 0)(lambda m=m, put=put: put(out_refs[m + half], out_refs[m]))
                pl.when(top == 1)(lambda m=m, put=put: put(out_refs[m], out_refs[m + half]))


def cross_packed(got, other, rows, cols, chans, windows):
    tiles = got[0].shape[0]
    size = 2 * cols * chans * rows * chans
    piece = jax.ShapeDtypeStruct((tiles, size, LANES), jnp.bfloat16)
    return pl.pallas_call(
        functools.partial(cross_kernel, rows=rows, chans=chans, tiles=tiles, windows=windows),
        out_shape=[piece] * rows,
        in_specs=[pl.BlockSpec(memory_space=pltpu.VMEM)] * (2 * rows),
        out_specs=[pl.BlockSpec(memory_space=pltpu.VMEM)] * rows,
        scratch_shapes=[
            pltpu.VMEM((3, tiles, windows * rows * chans, LANES), jnp.float32),
            pltpu.VMEM((2, rows, tiles, chans, 3, windows, LANES), jnp.float32),
        ],
        compiler_params=pltpu.CompilerParams(vmem_limit_bytes=32 * 2**20),
        cost_estimate=pl.CostEstimate(flops=10**9, bytes_accessed=2**20, transcendentals=0),
        name="cross",
    )(*got, *other)


def finish_kernel(*refs, rows, chans):
    got, out_ref, wide_ref = refs[:rows], refs[rows], refs[rows + 1]
    bands, _, firsts, quads, _, _ = out_ref.shape
    row, col = lax.axis_index("row"), lax.axis_index("col")
    per_row = 2 * chans
    second = row * per_row + lax.broadcasted_iota(jnp.int32, (SUB, LANES), 0) % per_row
    for n in range(rows):
        place = row ^ n
        b, c = place // quads, place % quads
        for t in range(2):
            for q in range(2):
                for s in range(2):
                    half = col if s == 0 else 1 - col
                    for k in range(chans):
                        spot = ((q * 2 + s) * chans + k) * firsts
                        to = pl.multiple_of(
                            (q * SUB + t * per_row + half * chans + k) * firsts, firsts
                        )
                        wide_ref[n, pl.ds(to, firsts), :] = got[n][
                            t, spot : spot + firsts, :
                        ].astype(jnp.float32)
        for q in range(2):
            for i in range(firsts):
                first = i // chans * per_row + col * chans + i % chans
                vals = wide_ref[n, pl.ds(q * SUB * firsts + i, SUB, stride=firsts), :]
                out_ref[b, q, i, c] = jnp.where(first <= second, vals, 0.0)


def finish_packed(got, bands, bins, rows, cols, chans):
    chunks = bins // LANES
    firsts = rows * chans
    out = pl.pallas_call(
        functools.partial(finish_kernel, rows=rows, chans=chans),
        out_shape=jax.ShapeDtypeStruct((bands, 2, firsts, chunks // 2, SUB, LANES), jnp.float32),
        in_specs=[pl.BlockSpec(memory_space=pltpu.VMEM)] * rows,
        out_specs=pl.BlockSpec(memory_space=pltpu.VMEM),
        scratch_shapes=[pltpu.VMEM((rows, 2 * SUB * firsts, LANES), jnp.float32)],
        compiler_params=pltpu.CompilerParams(vmem_limit_bytes=32 * 2**20),
        cost_estimate=pl.CostEstimate(flops=10**9, bytes_accessed=2**20, transcendentals=0),
        name="finish",
    )(*got)
    out = out.reshape(bands, 2, firsts, chunks, cols * chans, LANES)
    out = out.transpose(0, 1, 2, 4, 3, 5)
    return out.reshape(bands, 2, 1, firsts, cols * chans, bins)


def to_row(value, n, rows):
    return lax.ppermute(value, "row", [(r, r ^ n) for r in range(rows)])


def on_device_packed(spectra, window_flags):
    bands, windows, _, chans, bins = spectra.shape
    rows, cols = lax.axis_size("row"), lax.axis_size("col")
    order = sorted(range(1, rows), reverse=True)
    pieces = whiten_packed(spectra, window_flags, rows)
    got = [pieces[0]] * rows
    for n in order:
        got[n] = to_row(pieces[n], n, rows)
    other = [lax.ppermute(g, "col", [(0, 1), (1, 0)]) for g in got]
    result = cross_packed(got, other, rows, cols, chans, windows)
    back = [result[0]] * rows
    for n in order:
        back[n] = to_row(result[n], n, rows)
    return finish_packed(back, bands, bins, rows, cols, chans)


def on_device(spectra, window_flags):
    bands, windows, _, chans, bins = spectra.shape
    rows, cols = lax.axis_size("row"), lax.axis_size("col")
    if (
        bands * bins == rows * 2 * LANES
        and bins % (2 * LANES) == 0
        and rows in (2, 4, 8)
        and cols == 2
        and chans == 2
        and rows * chans == 2 * SUB
        and windows % 16 == 0
    ):
        return on_device_packed(spectra, window_flags)
    payload = whiten_plain(spectra, window_flags, rows * cols)
    got = lax.all_to_all(payload, ("row", "col"), 0, 0, tiled=True)
    result = cross_plain(got, rows, cols, chans, windows)
    back = lax.all_to_all(result, ("row", "col"), 0, 0, tiled=True)
    return finish_plain(back, bands, bins, rows, cols, chans)


def solution(mesh):
    in_specs = (P("parts", None, None, ("row", "col"), None), P("parts", ("row", "col")))
    out_specs = P("parts", None, "col", None, "row", None)
    return jax.shard_map(
        on_device, mesh=mesh, in_specs=in_specs, out_specs=out_specs, check_vma=False
    )
```

```python
import functools

import jax
import jax.numpy as jnp
from jax import lax
from jax.experimental import pallas as pl
from jax.experimental.pallas import tpu as pltpu
from jax.sharding import PartitionSpec as P

HALFWIN = 64
LANES = 128
SUB = 8

epsilon = 1e-06


def window_mean(magnitude):
    bins = magnitude.shape[-1]
    lead = [(0, 0)] * (magnitude.ndim - 1)
    padded = jnp.pad(magnitude, lead + [(HALFWIN + 1, HALFWIN)])
    running = jnp.cumsum(padded, axis=-1)
    total = running[..., 2 * HALFWIN + 1 :] - running[..., :bins]
    positions = jnp.arange(bins, dtype=jnp.int32)
    counted = (
        jnp.minimum(positions + HALFWIN, bins - 1) - jnp.maximum(positions - HALFWIN, 0) + 1
    ).astype(jnp.float32)
    return total / counted


def whiten_plain(spectra, window_flags, devices):
    bands, windows, parts, chans, bins = spectra.shape
    flags = window_flags.astype(jnp.float32)[None, :, None, :, None]
    values = spectra.astype(jnp.float32) * flags
    magnitude = jnp.sqrt(values[:, :, 0] * values[:, :, 0] + values[:, :, 1] * values[:, :, 1])
    smooth = window_mean(magnitude)
    white = (values / (smooth[:, :, None] + epsilon)).astype(jnp.bfloat16)
    own = bands * bins // devices
    white = white.reshape(bands, windows, parts, chans, bins // own, own)
    white = white.transpose(0, 4, 3, 2, 1, 5)
    return white.reshape(devices, chans * parts * windows, own)


def cross_plain(got, rows, cols, chans, windows):
    own = got.shape[-1]
    data = got.reshape(rows * cols * chans, 2, windows, own)
    prods = jnp.einsum("apwf,jqwf->pqajf", data, data, preferred_element_type=jnp.float32)
    both = jnp.stack([prods[0, 0] + prods[1, 1], prods[1, 0] - prods[0, 1]])
    both = both.reshape(2, rows, cols, chans, rows, cols * chans, own)
    both = both.transpose(4, 2, 0, 1, 3, 5, 6).astype(jnp.bfloat16)
    return both.reshape(rows * cols, 2 * rows * chans * cols * chans, own)


def finish_plain(got, bands, bins, rows, cols, chans):
    own = got.shape[-1]
    row, col = lax.axis_index("row"), lax.axis_index("col")
    data = got.reshape(bands, bins // own, 2, rows * chans, cols * chans, own)
    data = data.transpose(0, 2, 3, 4, 1, 5).reshape(
        bands, 2, rows * chans, cols * chans, bins
    )
    slot = jnp.arange(rows * chans, dtype=jnp.int32)
    first = (slot // chans * cols + col) * chans + slot % chans
    second = row * cols * chans + jnp.arange(cols * chans, dtype=jnp.int32)
    keep = (first[:, None] <= second[None, :])[:, :, None]
    return jnp.where(keep, data.astype(jnp.float32), 0.0)[:, :, None]


TILES = 2
VMEM_FIRST = 65454080


def whiten_kernel(flags_hbm, x_hbm, out_ref, flags_ref, x_ref, white_ref, sems, *, chans):
    bands, windows, _, group, _ = x_ref.shape
    chunks = group // chans
    step = 16
    steps = windows // step
    rows = step * group

    copies = [pltpu.make_async_copy(flags_hbm, flags_ref, sems.at[bands * steps])]
    for n in range(bands * steps):
        part = (n // steps, pl.ds(n % steps * step, step))
        copies.append(pltpu.make_async_copy(x_hbm.at[part], x_ref.at[part], sems.at[n]))
    for copy in copies:
        copy.start()

    row_id = lax.broadcasted_iota(jnp.int32, (rows, LANES), 0) % group
    lane_id = lax.broadcasted_iota(jnp.int32, (rows, LANES), 1)
    spot = row_id // chans * LANES + lane_id
    last = chunks * LANES - 1
    counted = jnp.minimum(spot + HALFWIN, last) - jnp.maximum(spot - HALFWIN, 0) + 1
    inv_count = 1.0 / counted.astype(jnp.float32)
    has_prev = row_id >= chans
    has_next = row_id < group - chans
    k_id = lax.broadcasted_iota(jnp.int32, (group, LANES), 0) % chans
    src = lax.broadcasted_iota(jnp.int32, (LANES, 3 * LANES), 0)
    dst = lax.broadcasted_iota(jnp.int32, (LANES, 3 * LANES), 1) - LANES
    band_mat = jnp.where(jnp.abs(src - dst) <= HALFWIN, 1.0, 0.0).astype(jnp.bfloat16)

    copies[0].wait()
    for b in range(bands):
        for n in range(steps):
            w0 = n * step
            copies[1 + b * steps + n].wait()
            x = x_ref[b, w0 : w0 + step].astype(jnp.float32)
            keeps = []
            for s in range(step):
                keep = jnp.full((group, LANES), flags_ref[0, w0 + s], jnp.int32)
                for k in range(1, chans):
                    keep = jnp.where(k_id == k, flags_ref[k, w0 + s], keep)
                keeps.append(keep)
            keep = jnp.stack(keeps).astype(jnp.float32)
            re = (x[:, 0] * keep).reshape(rows, LANES)
            im = (x[:, 1] * keep).reshape(rows, LANES)
            mag = jnp.sqrt(re * re + im * im)
            high = mag.astype(jnp.bfloat16)
            rest = (mag - high.astype(jnp.float32)).astype(jnp.bfloat16)
            sums = jnp.dot(high, band_mat, preferred_element_type=jnp.float32) + jnp.dot(
                rest, band_mat, preferred_element_type=jnp.float32
            )
            total = sums[:, LANES : 2 * LANES]
            total += jnp.where(has_prev, pltpu.roll(sums[:, 2 * LANES :], chans, 0), 0.0)
            total += jnp.where(has_next, pltpu.roll(sums[:, :LANES], rows - chans, 0), 0.0)
            inv = 1.0 / (total * inv_count + epsilon)
            for p, part in enumerate((re, im)):
                start = ((b * 2 + p) * windows + w0) * group
                white_ref[start : start + rows, :] = part * inv
        for c in range(chunks):
            for k in range(chans):
                for p in range(2):
                    start = (b * 2 + p) * windows * group + c * chans + k
                    slab = white_ref[pl.ds(start, windows, stride=group), :]
                    at = (k * 2 + p) * windows
                    out_ref[b * chunks + c, at : at + windows, :] = slab.astype(jnp.bfloat16)


def whiten_packed(view, flags):
    bands, windows, parts, group, _ = view.shape
    chans = flags.shape[0]
    tiles = bands * group // chans
    hbm = pl.BlockSpec(memory_space=pltpu.HBM)
    return pl.pallas_call(
        functools.partial(whiten_kernel, chans=chans),
        out_shape=jax.ShapeDtypeStruct((tiles, chans * parts * windows, LANES), jnp.bfloat16),
        in_specs=[hbm, hbm],
        out_specs=pl.BlockSpec(memory_space=pltpu.VMEM),
        scratch_shapes=[
            pltpu.SMEM(flags.shape, jnp.int32),
            pltpu.VMEM(view.shape, jnp.bfloat16),
            pltpu.VMEM((bands * parts * windows * group, LANES), jnp.float32),
            pltpu.SemaphoreType.DMA((bands * windows // 16 + 1,)),
        ],
        compiler_params=pltpu.CompilerParams(vmem_limit_bytes=VMEM_FIRST),
        cost_estimate=pl.CostEstimate(flops=10**9, bytes_accessed=2**20, transcendentals=0),
        name="whiten",
    )(flags, view)


def spread_second(second_ref, values, windows, chans):
    for k in range(chans):
        row = k * 2 * windows
        re = values[row : row + windows].astype(jnp.float32)
        im = values[row + windows : row + 2 * windows].astype(jnp.float32)
        second_ref[k, 0] = re
        second_ref[k, 1] = im - re
        second_ref[k, 2] = re + im


def spread_first(first_ref, row_at, values, windows, chans):
    for k in range(chans):
        row = k * 2 * windows
        re = values[row : row + windows].astype(jnp.float32)
        im = values[row + windows : row + 2 * windows].astype(jnp.float32)
        slot = pl.ds(row_at * chans + k, windows, stride=SUB)
        first_ref[0, slot, :] = re + im
        first_ref[1, slot, :] = im
        first_ref[2, slot, :] = re


def pair_sums(work, windows):
    zero = jnp.zeros((SUB, LANES), jnp.float32)

    def body(w, sums):
        base = pl.multiple_of(w * SUB, SUB)
        loaded = {}

        def load(ref, at):
            if id(ref) not in loaded:
                loaded[id(ref)] = [ref[q, at, :] for q in range(3)]
            return loaded[id(ref)]

        out = []
        for (first_ref, second_ref), (s1, s2, s3) in zip(work, sums):
            f = load(first_ref, pl.ds(base, SUB))
            g = load(second_ref, pl.ds(w, 1))
            out.append((s1 + g[0] * f[0], s2 + g[1] * f[1], s3 + g[2] * f[2]))
        return tuple(out)

    sums = lax.fori_loop(0, windows, body, ((zero, zero, zero),) * len(work), unroll=8)
    return [(s1 + s2, s1 - s3) for s1, s2, s3 in sums]


def far_sums(first_ref, values_ref, second_ref, put, rows, chans, windows):
    low = lax.broadcasted_iota(jnp.int32, (SUB, LANES), 0) < SUB // 2
    for t in range(TILES):
        firsts = [first_ref.at[block, t] for block in range(2)]
        seconds = {}
        for r in range(2, rows):
            spread_second(second_ref.at[t, r], values_ref[r * TILES + t], windows, chans)
            seconds[r] = [second_ref.at[t, r, k] for k in range(chans)]
        mid = range(2, rows - 2)
        sums = pair_sums([(firsts[0], g) for r in mid for g in seconds[r]], windows)
        for n, r in enumerate(mid):
            for q in range(2):
                vals = jnp.concatenate([sums[n * chans + k][q] for k in range(chans)])
                put(r, t, q * chans * SUB, vals)
        last = range(rows - 2, rows)
        sums = pair_sums([(f, g) for r in last for g in seconds[r] for f in firsts], windows)
        for n, r in enumerate(last):
            mine = sums[n * 2 * chans : (n + 1) * 2 * chans]
            rest = []
            for q in range(2):
                vals = jnp.concatenate([mine[k * 2][q] for k in range(chans)])
                put(r, t, q * chans * SUB, vals)
                rest.append(jnp.where(low, mine[1][q], pltpu.roll(mine[3][q], SUB // 2, 0)))
            put(r, t, 2 * chans * SUB, jnp.concatenate(rest))


def far_own_kernel(got_ref, first_ref, out_ref, second_ref, *, rows, chans, windows):
    for t in range(TILES):
        for r in range(rows - 2):
            spread_first(
                first_ref.at[r * chans // SUB, t],
                r % (SUB // chans),
                got_ref[r * TILES + t],
                windows,
                chans,
            )

    def put(r, t, at, vals):
        out_ref[r * TILES + t, at : at + 2 * SUB, :] = vals.astype(jnp.bfloat16)

    far_sums(first_ref, got_ref, second_ref, put, rows, chans, windows)


def far_other_kernel(other_ref, first_ref, own_ref, out_ref, second_ref, *, rows, chans, windows):
    size = own_ref.shape[1]
    out_ref[: 2 * TILES] = jnp.zeros((2 * TILES, *out_ref.shape[1:]), out_ref.dtype)
    mid = pl.ds(2 * TILES, (rows - 4) * TILES)
    rest = jnp.zeros(((rows - 4) * TILES, 2 * SUB, LANES), out_ref.dtype)
    out_ref[2 * TILES :, :size, :] = own_ref[2 * TILES :]
    for s in range(2):
        out_ref[mid, s * size + 4 * SUB : s * size + 6 * SUB, :] = rest

    def put(r, t, at, vals):
        at += size
        out_ref[r * TILES + t, at : at + 2 * SUB, :] = vals.astype(jnp.bfloat16)

    far_sums(first_ref, other_ref, second_ref, put, rows, chans, windows)


def far_packed(got, swap, rows, chans, windows):
    vmem = pl.BlockSpec(memory_space=pltpu.VMEM)
    params = dict(
        scratch_shapes=[pltpu.VMEM((TILES, rows, chans, 3, windows, LANES), jnp.float32)],
        compiler_params=pltpu.CompilerParams(vmem_limit_bytes=32 * 2**20),
        cost_estimate=pl.CostEstimate(flops=10**9, bytes_accessed=2**20, transcendentals=0),
    )
    size = 3 * chans * SUB
    sizes = dict(rows=rows, chans=chans, windows=windows)
    first, own = pl.pallas_call(
        functools.partial(far_own_kernel, **sizes),
        out_shape=[
            jax.ShapeDtypeStruct((2, TILES, 3, windows * SUB, LANES), jnp.float32),
            jax.ShapeDtypeStruct((rows * TILES, size, LANES), jnp.bfloat16),
        ],
        in_specs=[vmem],
        out_specs=[vmem] * 2,
        name="far_own",
        **params,
    )(got)
    return pl.pallas_call(
        functools.partial(far_other_kernel, **sizes),
        out_shape=jax.ShapeDtypeStruct((rows * TILES, 2 * size, LANES), jnp.bfloat16),
        in_specs=[vmem] * 3,
        out_specs=vmem,
        name="far_other",
        **params,
    )(swap(got), first, own)


def halves_kernel(own_ref, keep_ref, give_ref):
    odd = lax.axis_index("row") % 2
    tiles = keep_ref.shape[0]
    keep_ref[...] = own_ref[pl.ds(odd * tiles, tiles)]
    give_ref[...] = own_ref[pl.ds((1 - odd) * tiles, tiles)]


def halves_packed(own):
    vmem = pl.BlockSpec(memory_space=pltpu.VMEM)
    band = jax.ShapeDtypeStruct((own.shape[0] // 2, *own.shape[1:]), own.dtype)
    return pl.pallas_call(
        halves_kernel,
        out_shape=[band] * 2,
        in_specs=[vmem],
        out_specs=[vmem] * 2,
        compiler_params=pltpu.CompilerParams(vmem_limit_bytes=32 * 2**20),
        cost_estimate=pl.CostEstimate(flops=10**9, bytes_accessed=2**20, transcendentals=0),
        name="halves",
    )(own)


def near_kernel(*refs, windows):
    sources, outs, (first_ref, second_ref) = refs[:4], refs[4:6], refs[6:]
    chans = 2
    odd = lax.axis_index("row") % 2
    low = lax.broadcasted_iota(jnp.int32, (SUB, LANES), 0) < SUB // 2
    tiles = outs[0].shape[0]

    def body(m, carry):
        for t in range(TILES):
            tile = m * TILES + t
            first = first_ref.at[t]
            work = []
            for n in range(2):
                own_ref, other_ref = sources[2 * n : 2 * n + 2]
                spread_first(first, odd if n == 0 else 1 - odd, own_ref[tile], windows, chans)
                for s, ref in enumerate((own_ref, other_ref)):
                    spread_second(second_ref.at[t, n, s], ref[tile], windows, chans)
                    work += [(first, second_ref.at[t, n, s, k]) for k in range(chans)]
            sums = pair_sums(work, windows)
            for n, out_ref in enumerate(outs):
                for s in range(2):
                    one, two = sums[(n * 2 + s) * chans : (n * 2 + s + 1) * chans]
                    vals = [
                        jnp.where(low, one[q], pltpu.roll(two[q], SUB // 2, 0)) for q in range(2)
                    ]
                    vals = jnp.concatenate(vals).astype(jnp.bfloat16)
                    out_ref[tile, s * 2 * SUB : (s + 1) * 2 * SUB, :] = vals
        return carry

    lax.fori_loop(0, tiles // TILES, body, 0)


def near_packed(keep, keep_other, took, took_other, windows):
    vmem = pl.BlockSpec(memory_space=pltpu.VMEM)
    piece = jax.ShapeDtypeStruct((keep.shape[0], 4 * SUB, LANES), jnp.bfloat16)
    return pl.pallas_call(
        functools.partial(near_kernel, windows=windows),
        out_shape=[piece] * 2,
        in_specs=[vmem] * 4,
        out_specs=[vmem] * 2,
        scratch_shapes=[
            pltpu.VMEM((TILES, 3, windows * SUB, LANES), jnp.float32),
            pltpu.VMEM((TILES, 2, 2, 2, 3, windows, LANES), jnp.float32),
        ],
        compiler_params=pltpu.CompilerParams(vmem_limit_bytes=32 * 2**20),
        cost_estimate=pl.CostEstimate(flops=10**9, bytes_accessed=2**20, transcendentals=0),
        name="near",
    )(keep, keep_other, took, took_other)


def finish_kernel(far_ref, kept_ref, taken_ref, out_ref, wide_ref, near_ref, *, rows, chans):
    level, odd = lax.axis_index("row") // 2, lax.axis_index("row") % 2
    col = lax.axis_index("col")
    per_row = 2 * chans
    firsts = rows * chans
    half = rows // 2
    size = 3 * chans * SUB
    for r in range(rows):
        for t in range(TILES):
            for s in range(2):
                side = col if s == 0 else 1 - col
                rest = far_ref[r * TILES + t, s * size + 4 * SUB : (s + 1) * size, :]
                rest = rest.astype(jnp.float32)
                for q in range(2):
                    spot = s * size + q * chans * SUB
                    vals = far_ref[r * TILES + t, spot : spot + chans * SUB, :]
                    vals = vals.astype(jnp.float32)
                    more = rest[q * SUB : (q + 1) * SUB]
                    for k in range(chans):
                        to = (q * SUB + t * per_row + side * chans + k) * firsts
                        to = pl.multiple_of(to, firsts)
                        wide_ref[r, pl.ds(to, SUB), :] = vals[k * SUB : (k + 1) * SUB]
                        tail = more if k == 0 else pltpu.roll(more, SUB // 2, 0)
                        wide_ref[r, pl.ds(to + SUB, SUB), :] = tail
    for r in range(rows):
        for q in range(2):
            for i in range(firsts):
                if i < firsts - per_row:
                    vals = wide_ref[r, pl.ds(q * SUB * firsts + i, SUB, stride=firsts), :]
                    keep = jnp.full((SUB, LANES), level, jnp.int32) > i // per_row
                    vals = jnp.where(keep, vals, 0.0)
                else:
                    vals = jnp.zeros((SUB, LANES), jnp.float32)
                out_ref[r // half, q, i, r % half] = vals
    second = odd * per_row + lax.broadcasted_iota(jnp.int32, (SUB, LANES), 0) % per_row
    for n, ref in enumerate((kept_ref, taken_ref)):
        for m in range(half):
            for t in range(TILES):
                for s in range(2):
                    side = col if s == 0 else 1 - col
                    vals = ref[m * TILES + t, s * 2 * SUB : (s + 1) * 2 * SUB, :]
                    vals = vals.astype(jnp.float32)
                    for q in range(2):
                        for k in range(chans):
                            to = (q * SUB + t * per_row + side * chans + k) * SUB
                            part = vals[q * SUB : (q + 1) * SUB]
                            part = part if k == 0 else pltpu.roll(part, SUB // 2, 0)
                            near_ref[n, m, pl.ds(pl.multiple_of(to, SUB), SUB), :] = part
    for n in range(2):
        band = odd if n == 0 else 1 - odd
        for m in range(half):
            for q in range(2):
                for i in range(per_row):
                    first = i // chans * per_row + col * chans + i % chans
                    vals = near_ref[n, m, pl.ds(q * SUB * SUB + i, SUB, stride=SUB), :]
                    out_ref[band, q, level * per_row + i, m] = jnp.where(first <= second, vals, 0.0)


def finish_packed(far, kept, taken, rows, chans):
    vmem = pl.BlockSpec(memory_space=pltpu.VMEM)
    firsts = rows * chans
    return pl.pallas_call(
        functools.partial(finish_kernel, rows=rows, chans=chans),
        out_shape=jax.ShapeDtypeStruct((2, 2, firsts, rows // 2, SUB, LANES), jnp.float32),
        in_specs=[vmem] * 3,
        out_specs=vmem,
        scratch_shapes=[
            pltpu.VMEM((rows, 2 * SUB * firsts, LANES), jnp.float32),
            pltpu.VMEM((2, rows // 2, 2 * SUB * SUB, LANES), jnp.float32),
        ],
        compiler_params=pltpu.CompilerParams(vmem_limit_bytes=32 * 2**20),
        cost_estimate=pl.CostEstimate(flops=10**9, bytes_accessed=2**20, transcendentals=0),
        name="finish",
    )(far, kept, taken)


def on_device_packed(spectra, window_flags):
    bands, windows, parts, chans, bins = spectra.shape
    rows, cols = lax.axis_size("row"), lax.axis_size("col")
    chunks = bins // LANES
    view = spectra.reshape(bands, windows, parts, chans, chunks, LANES)
    view = view.transpose(0, 1, 2, 4, 3, 5).reshape(bands, windows, parts, chunks * chans, LANES)

    def swap(value):
        return lax.ppermute(value, "col", [(0, 1), (1, 0)])

    own = whiten_packed(view, window_flags.T)
    got = lax.all_to_all(own, "row", 0, 0, tiled=True)

    def level_swap(value):
        return lax.ppermute(value, "row", [(r, r ^ 1) for r in range(rows)])

    keep, give = halves_packed(own)
    took = level_swap(give)
    got, took = lax.optimization_barrier((got, took))
    far = far_packed(got, swap, rows, chans, windows)
    far = lax.all_to_all(far, "row", 0, 0, tiled=True)
    kept, give = near_packed(keep, swap(keep), took, swap(took), windows)
    out = finish_packed(far, kept, level_swap(give), rows, chans)
    out = out.reshape(bands, 2, rows * chans, chunks, cols * chans, LANES)
    out = out.transpose(0, 1, 2, 4, 3, 5)
    return out.reshape(bands, 2, 1, rows * chans, cols * chans, bins)


def on_device(spectra, window_flags):
    bands, windows, _, chans, bins = spectra.shape
    rows, cols = lax.axis_size("row"), lax.axis_size("col")
    if (
        bands == 2
        and rows == 8
        and bands * bins == rows * TILES * LANES
        and cols == 2
        and chans == 2
        and windows % 16 == 0
        and bins == rows * LANES
    ):
        return on_device_packed(spectra, window_flags)
    payload = whiten_plain(spectra, window_flags, rows * cols)
    got = lax.all_to_all(payload, ("row", "col"), 0, 0, tiled=True)
    result = cross_plain(got, rows, cols, chans, windows)
    back = lax.all_to_all(result, ("row", "col"), 0, 0, tiled=True)
    return finish_plain(back, bands, bins, rows, cols, chans)


def solution(mesh):
    in_specs = (P("parts", None, None, ("row", "col"), None), P("parts", ("row", "col")))
    out_specs = P("parts", None, "col", None, "row", None)
    return jax.shard_map(
        on_device, mesh=mesh, in_specs=in_specs, out_specs=out_specs, check_vma=False
    )
```

```python
import functools

import jax
import jax.numpy as jnp
from jax import lax
from jax.experimental import pallas as pl
from jax.experimental.pallas import tpu as pltpu
from jax.sharding import PartitionSpec as P

HALFWIN = 64
LANES = 128
SUB = 8

epsilon = 1e-06


def window_mean(magnitude):
    bins = magnitude.shape[-1]
    lead = [(0, 0)] * (magnitude.ndim - 1)
    padded = jnp.pad(magnitude, lead + [(HALFWIN + 1, HALFWIN)])
    running = jnp.cumsum(padded, axis=-1)
    total = running[..., 2 * HALFWIN + 1 :] - running[..., :bins]
    positions = jnp.arange(bins, dtype=jnp.int32)
    counted = (
        jnp.minimum(positions + HALFWIN, bins - 1) - jnp.maximum(positions - HALFWIN, 0) + 1
    ).astype(jnp.float32)
    return total / counted


def whiten_plain(spectra, window_flags, devices):
    bands, windows, parts, chans, bins = spectra.shape
    flags = window_flags.astype(jnp.float32)[None, :, None, :, None]
    values = spectra.astype(jnp.float32) * flags
    magnitude = jnp.sqrt(values[:, :, 0] * values[:, :, 0] + values[:, :, 1] * values[:, :, 1])
    smooth = window_mean(magnitude)
    white = (values / (smooth[:, :, None] + epsilon)).astype(jnp.bfloat16)
    own = bands * bins // devices
    white = white.reshape(bands, windows, parts, chans, bins // own, own)
    white = white.transpose(0, 4, 3, 2, 1, 5)
    return white.reshape(devices, chans * parts * windows, own)


def cross_plain(got, rows, cols, chans, windows):
    own = got.shape[-1]
    data = got.reshape(rows * cols * chans, 2, windows, own)
    prods = jnp.einsum("apwf,jqwf->pqajf", data, data, preferred_element_type=jnp.float32)
    both = jnp.stack([prods[0, 0] + prods[1, 1], prods[1, 0] - prods[0, 1]])
    both = both.reshape(2, rows, cols, chans, rows, cols * chans, own)
    both = both.transpose(4, 2, 0, 1, 3, 5, 6).astype(jnp.bfloat16)
    return both.reshape(rows * cols, 2 * rows * chans * cols * chans, own)


def finish_plain(got, bands, bins, rows, cols, chans):
    own = got.shape[-1]
    row, col = lax.axis_index("row"), lax.axis_index("col")
    data = got.reshape(bands, bins // own, 2, rows * chans, cols * chans, own)
    data = data.transpose(0, 2, 3, 4, 1, 5).reshape(
        bands, 2, rows * chans, cols * chans, bins
    )
    slot = jnp.arange(rows * chans, dtype=jnp.int32)
    first = (slot // chans * cols + col) * chans + slot % chans
    second = row * cols * chans + jnp.arange(cols * chans, dtype=jnp.int32)
    keep = (first[:, None] <= second[None, :])[:, :, None]
    return jnp.where(keep, data.astype(jnp.float32), 0.0)[:, :, None]


TILES = 2
VMEM_FIRST = 65454080


def whiten_kernel(
    flags_hbm, x_hbm, out_hbm, flags_ref, x_ref, white_ref, out_ref, sems, out_sems, *, chans
):
    bands, windows, _, group, _ = x_ref.shape
    chunks = group // chans
    step = 16
    steps = windows // step
    rows = step * group

    copies = [pltpu.make_async_copy(flags_hbm, flags_ref, sems.at[bands * steps])]
    for n in range(bands * steps):
        part = (n // steps, pl.ds(n % steps * step, step))
        copies.append(pltpu.make_async_copy(x_hbm.at[part], x_ref.at[part], sems.at[n]))
    for copy in copies:
        copy.start()

    row_id = lax.broadcasted_iota(jnp.int32, (rows, LANES), 0) % group
    lane_id = lax.broadcasted_iota(jnp.int32, (rows, LANES), 1)
    spot = row_id // chans * LANES + lane_id
    last = chunks * LANES - 1
    counted = jnp.minimum(spot + HALFWIN, last) - jnp.maximum(spot - HALFWIN, 0) + 1
    inv_count = 1.0 / counted.astype(jnp.float32)
    has_prev = row_id >= chans
    has_next = row_id < group - chans
    k_id = lax.broadcasted_iota(jnp.int32, (group, LANES), 0) % chans
    src = lax.broadcasted_iota(jnp.int32, (LANES, 3 * LANES), 0)
    dst = lax.broadcasted_iota(jnp.int32, (LANES, 3 * LANES), 1) - LANES
    band_mat = jnp.where(jnp.abs(src - dst) <= HALFWIN, 1.0, 0.0).astype(jnp.bfloat16)

    copies[0].wait()
    for b in range(bands):
        for n in range(steps):
            w0 = n * step
            copies[1 + b * steps + n].wait()
            x = x_ref[b, w0 : w0 + step].astype(jnp.float32)
            keeps = []
            for s in range(step):
                keep = jnp.full((group, LANES), flags_ref[0, w0 + s], jnp.int32)
                for k in range(1, chans):
                    keep = jnp.where(k_id == k, flags_ref[k, w0 + s], keep)
                keeps.append(keep)
            keep = jnp.stack(keeps).astype(jnp.float32)
            re = (x[:, 0] * keep).reshape(rows, LANES)
            im = (x[:, 1] * keep).reshape(rows, LANES)
            mag = jnp.sqrt(re * re + im * im)
            high = mag.astype(jnp.bfloat16)
            rest = (mag - high.astype(jnp.float32)).astype(jnp.bfloat16)
            sums = jnp.dot(high, band_mat, preferred_element_type=jnp.float32) + jnp.dot(
                rest, band_mat, preferred_element_type=jnp.float32
            )
            total = sums[:, LANES : 2 * LANES]
            total += jnp.where(has_prev, pltpu.roll(sums[:, 2 * LANES :], chans, 0), 0.0)
            total += jnp.where(has_next, pltpu.roll(sums[:, :LANES], rows - chans, 0), 0.0)
            inv = 1.0 / (total * inv_count + epsilon)
            for p, part in enumerate((re, im)):
                start = ((b * 2 + p) * windows + w0) * group
                white_ref[start : start + rows, :] = part * inv
        for c in range(chunks):
            for k in range(chans):
                for p in range(2):
                    start = (b * 2 + p) * windows * group + c * chans + k
                    slab = white_ref[pl.ds(start, windows, stride=group), :]
                    at = (k * 2 + p) * windows
                    out_ref[b * chunks + c, at : at + windows, :] = slab.astype(jnp.bfloat16)
            if c % TILES == TILES - 1:
                n = (b * chunks + c) // TILES
                part = pl.ds(n * TILES, TILES)
                copy = pltpu.make_async_copy(out_ref.at[part], out_hbm.at[part], out_sems.at[n])
                copy.start()
                copies.append(copy)
    for copy in copies[1 + bands * steps :]:
        copy.wait()


def whiten_packed(view, flags):
    bands, windows, parts, group, _ = view.shape
    chans = flags.shape[0]
    tiles = bands * group // chans
    hbm = pl.BlockSpec(memory_space=pltpu.HBM)
    shape = (tiles, chans * parts * windows, LANES)
    return pl.pallas_call(
        functools.partial(whiten_kernel, chans=chans),
        out_shape=jax.ShapeDtypeStruct(shape, jnp.bfloat16),
        in_specs=[hbm, hbm],
        out_specs=hbm,
        scratch_shapes=[
            pltpu.SMEM(flags.shape, jnp.int32),
            pltpu.VMEM(view.shape, jnp.bfloat16),
            pltpu.VMEM((bands * parts * windows * group, LANES), jnp.float32),
            pltpu.VMEM(shape, jnp.bfloat16),
            pltpu.SemaphoreType.DMA((bands * windows // 16 + 1,)),
            pltpu.SemaphoreType.DMA((tiles // TILES,)),
        ],
        compiler_params=pltpu.CompilerParams(vmem_limit_bytes=VMEM_FIRST),
        cost_estimate=pl.CostEstimate(flops=10**9, bytes_accessed=2**20, transcendentals=0),
        name="whiten",
    )(flags, view)


def spread_second(second_ref, values, windows, chans):
    for k in range(chans):
        row = k * 2 * windows
        re = values[row : row + windows].astype(jnp.float32)
        im = values[row + windows : row + 2 * windows].astype(jnp.float32)
        second_ref[k, 0] = re
        second_ref[k, 1] = im - re
        second_ref[k, 2] = re + im


def spread_first(first_ref, row_at, values, windows, chans):
    for k in range(chans):
        row = k * 2 * windows
        re = values[row : row + windows].astype(jnp.float32)
        im = values[row + windows : row + 2 * windows].astype(jnp.float32)
        slot = pl.ds(row_at * chans + k, windows, stride=SUB)
        first_ref[0, slot, :] = re + im
        first_ref[1, slot, :] = im
        first_ref[2, slot, :] = re


def pair_sums(work, windows):
    zero = jnp.zeros((SUB, LANES), jnp.float32)

    def body(w, sums):
        base = pl.multiple_of(w * SUB, SUB)
        loaded = {}

        def load(ref, at):
            if id(ref) not in loaded:
                loaded[id(ref)] = [ref[q, at, :] for q in range(3)]
            return loaded[id(ref)]

        out = []
        for (first_ref, second_ref), (s1, s2, s3) in zip(work, sums):
            f = load(first_ref, pl.ds(base, SUB))
            g = load(second_ref, pl.ds(w, 1))
            out.append((s1 + g[0] * f[0], s2 + g[1] * f[1], s3 + g[2] * f[2]))
        return tuple(out)

    sums = lax.fori_loop(0, windows, body, ((zero, zero, zero),) * len(work), unroll=8)
    return [(s1 + s2, s1 - s3) for s1, s2, s3 in sums]


def far_sums(first_ref, values_ref, second_ref, put, rows, chans, windows, done=None):
    low = lax.broadcasted_iota(jnp.int32, (SUB, LANES), 0) < SUB // 2
    for t in range(TILES):
        firsts = [first_ref.at[block, t] for block in range(2)]
        seconds = {}
        for r in range(2, rows):
            spread_second(second_ref.at[t, r], values_ref[r * TILES + t], windows, chans)
            seconds[r] = [second_ref.at[t, r, k] for k in range(chans)]
        mid = range(2, rows - 2)
        sums = pair_sums([(firsts[0], g) for r in mid for g in seconds[r]], windows)
        for n, r in enumerate(mid):
            for q in range(2):
                vals = jnp.concatenate([sums[n * chans + k][q] for k in range(chans)])
                put(r, t, q * chans * SUB, vals)
        last = range(rows - 2, rows)
        sums = pair_sums([(f, g) for r in last for g in seconds[r] for f in firsts], windows)
        for n, r in enumerate(last):
            mine = sums[n * 2 * chans : (n + 1) * 2 * chans]
            rest = []
            for q in range(2):
                vals = jnp.concatenate([mine[k * 2][q] for k in range(chans)])
                put(r, t, q * chans * SUB, vals)
                rest.append(jnp.where(low, mine[1][q], pltpu.roll(mine[3][q], SUB // 2, 0)))
            put(r, t, 2 * chans * SUB, jnp.concatenate(rest))
        if done is not None:
            done(t)


def far_own_kernel(got_ref, first_ref, out_ref, second_ref, *, rows, chans, windows):
    for t in range(TILES):
        for r in range(rows - 2):
            spread_first(
                first_ref.at[r * chans // SUB, t],
                r % (SUB // chans),
                got_ref[r * TILES + t],
                windows,
                chans,
            )

    def put(r, t, at, vals):
        out_ref[r * TILES + t, at : at + 2 * SUB, :] = vals.astype(jnp.bfloat16)

    far_sums(first_ref, got_ref, second_ref, put, rows, chans, windows)


def far_other_kernel(
    other_ref, first_ref, own_ref, out_hbm, second_ref, out_ref, sems, *, rows, chans, windows
):
    size = own_ref.shape[1]
    copies = []

    def send(first, count):
        part = pl.ds(first, count)
        sem = sems.at[len(copies)]
        copies.append(pltpu.make_async_copy(out_ref.at[part], out_hbm.at[part], sem))
        copies[-1].start()

    out_ref[: 2 * TILES] = jnp.zeros((2 * TILES, *out_ref.shape[1:]), out_ref.dtype)
    send(0, 2 * TILES)
    mid = pl.ds(2 * TILES, (rows - 4) * TILES)
    rest = jnp.zeros(((rows - 4) * TILES, 2 * SUB, LANES), out_ref.dtype)
    out_ref[2 * TILES :, :size, :] = own_ref[2 * TILES :]
    for s in range(2):
        out_ref[mid, s * size + 4 * SUB : s * size + 6 * SUB, :] = rest

    def put(r, t, at, vals):
        at += size
        out_ref[r * TILES + t, at : at + 2 * SUB, :] = vals.astype(jnp.bfloat16)

    def done(t):
        for r in range(2, rows):
            send(r * TILES + t, 1)

    far_sums(first_ref, other_ref, second_ref, put, rows, chans, windows, done)
    for copy in copies:
        copy.wait()


def far_packed(got, swap, rows, chans, windows):
    vmem = pl.BlockSpec(memory_space=pltpu.VMEM)
    scratch = [pltpu.VMEM((TILES, rows, chans, 3, windows, LANES), jnp.float32)]
    params = dict(
        compiler_params=pltpu.CompilerParams(vmem_limit_bytes=32 * 2**20),
        cost_estimate=pl.CostEstimate(flops=10**9, bytes_accessed=2**20, transcendentals=0),
    )
    size = 3 * chans * SUB
    sizes = dict(rows=rows, chans=chans, windows=windows)
    first, own = pl.pallas_call(
        functools.partial(far_own_kernel, **sizes),
        out_shape=[
            jax.ShapeDtypeStruct((2, TILES, 3, windows * SUB, LANES), jnp.float32),
            jax.ShapeDtypeStruct((rows * TILES, size, LANES), jnp.bfloat16),
        ],
        in_specs=[vmem],
        out_specs=[vmem] * 2,
        scratch_shapes=scratch,
        name="far_own",
        **params,
    )(got)
    return pl.pallas_call(
        functools.partial(far_other_kernel, **sizes),
        out_shape=jax.ShapeDtypeStruct((rows * TILES, 2 * size, LANES), jnp.bfloat16),
        in_specs=[vmem] * 3,
        out_specs=pl.BlockSpec(memory_space=pltpu.HBM),
        scratch_shapes=scratch
        + [
            pltpu.VMEM((rows * TILES, 2 * size, LANES), jnp.bfloat16),
            pltpu.SemaphoreType.DMA((1 + (rows - 2) * TILES,)),
        ],
        name="far_other",
        **params,
    )(swap(got), first, own)


def halves_kernel(own_ref, keep_ref, give_ref):
    odd = lax.axis_index("row") % 2
    tiles = keep_ref.shape[0]
    keep_ref[...] = own_ref[pl.ds(odd * tiles, tiles)]
    give_ref[...] = own_ref[pl.ds((1 - odd) * tiles, tiles)]


def halves_packed(own):
    vmem = pl.BlockSpec(memory_space=pltpu.VMEM)
    band = jax.ShapeDtypeStruct((own.shape[0] // 2, *own.shape[1:]), own.dtype)
    return pl.pallas_call(
        halves_kernel,
        out_shape=[band] * 2,
        in_specs=[vmem],
        out_specs=[vmem] * 2,
        compiler_params=pltpu.CompilerParams(vmem_limit_bytes=32 * 2**20),
        cost_estimate=pl.CostEstimate(flops=10**9, bytes_accessed=2**20, transcendentals=0),
        name="halves",
    )(own)


def near_kernel(*refs, windows):
    sources, outs, (first_ref, second_ref) = refs[:4], refs[4:6], refs[6:]
    chans = 2
    odd = lax.axis_index("row") % 2
    low = lax.broadcasted_iota(jnp.int32, (SUB, LANES), 0) < SUB // 2
    tiles = outs[0].shape[0]

    def body(m, carry):
        for t in range(TILES):
            tile = m * TILES + t
            first = first_ref.at[t]
            work = []
            for n in range(2):
                own_ref, other_ref = sources[2 * n : 2 * n + 2]
                spread_first(first, odd if n == 0 else 1 - odd, own_ref[tile], windows, chans)
                for s, ref in enumerate((own_ref, other_ref)):
                    spread_second(second_ref.at[t, n, s], ref[tile], windows, chans)
                    work += [(first, second_ref.at[t, n, s, k]) for k in range(chans)]
            sums = pair_sums(work, windows)
            for n, out_ref in enumerate(outs):
                for s in range(2):
                    one, two = sums[(n * 2 + s) * chans : (n * 2 + s + 1) * chans]
                    vals = [
                        jnp.where(low, one[q], pltpu.roll(two[q], SUB // 2, 0)) for q in range(2)
                    ]
                    vals = jnp.concatenate(vals).astype(jnp.bfloat16)
                    out_ref[tile, s * 2 * SUB : (s + 1) * 2 * SUB, :] = vals
        return carry

    lax.fori_loop(0, tiles // TILES, body, 0)


def near_packed(keep, keep_other, took, took_other, windows):
    vmem = pl.BlockSpec(memory_space=pltpu.VMEM)
    piece = jax.ShapeDtypeStruct((keep.shape[0], 4 * SUB, LANES), jnp.bfloat16)
    return pl.pallas_call(
        functools.partial(near_kernel, windows=windows),
        out_shape=[piece] * 2,
        in_specs=[vmem] * 4,
        out_specs=[vmem] * 2,
        scratch_shapes=[
            pltpu.VMEM((TILES, 3, windows * SUB, LANES), jnp.float32),
            pltpu.VMEM((TILES, 2, 2, 2, 3, windows, LANES), jnp.float32),
        ],
        compiler_params=pltpu.CompilerParams(vmem_limit_bytes=32 * 2**20),
        cost_estimate=pl.CostEstimate(flops=10**9, bytes_accessed=2**20, transcendentals=0),
        name="near",
    )(keep, keep_other, took, took_other)


def near_out_kernel(kept_ref, taken_ref, out_hbm, wide_ref, out_ref, sems, *, chans):
    level, odd = lax.axis_index("row") // 2, lax.axis_index("row") % 2
    col = lax.axis_index("col")
    per_row = 2 * chans
    bands, parts, _, quads, _, _ = out_ref.shape
    second = odd * per_row + lax.broadcasted_iota(jnp.int32, (SUB, LANES), 0) % per_row
    for n, ref in enumerate((kept_ref, taken_ref)):
        for m in range(quads):
            for t in range(TILES):
                for s in range(2):
                    side = col if s == 0 else 1 - col
                    vals = ref[m * TILES + t, s * 2 * SUB : (s + 1) * 2 * SUB, :]
                    vals = vals.astype(jnp.float32)
                    for q in range(parts):
                        for k in range(chans):
                            to = (q * SUB + t * per_row + side * chans + k) * SUB
                            part = vals[q * SUB : (q + 1) * SUB]
                            part = part if k == 0 else pltpu.roll(part, SUB // 2, 0)
                            wide_ref[n, m, pl.ds(pl.multiple_of(to, SUB), SUB), :] = part
    copies = []
    for b in range(bands):
        for q in range(parts):
            out_ref[b, q] = jnp.zeros(out_ref.shape[2:], out_ref.dtype)
            for m in range(quads):
                for i in range(per_row):
                    first = i // chans * per_row + col * chans + i % chans
                    spot = pl.ds(q * SUB * SUB + i, SUB, stride=SUB)
                    vals = wide_ref[b ^ odd, m, spot, :]
                    out_ref[b, q, level * per_row + i, m] = jnp.where(first <= second, vals, 0.0)
            sem = sems.at[b * parts + q]
            copies.append(pltpu.make_async_copy(out_ref.at[b, q], out_hbm.at[b, q], sem))
            copies[-1].start()
    for copy in copies:
        copy.wait()


def near_out_packed(kept, taken, rows, chans):
    vmem = pl.BlockSpec(memory_space=pltpu.VMEM)
    shape = (2, 2, rows * chans, rows // 2, SUB, LANES)
    return pl.pallas_call(
        functools.partial(near_out_kernel, chans=chans),
        out_shape=jax.ShapeDtypeStruct(shape, jnp.float32),
        in_specs=[vmem] * 2,
        out_specs=pl.BlockSpec(memory_space=pltpu.HBM),
        scratch_shapes=[
            pltpu.VMEM((2, rows // 2, 2 * SUB * SUB, LANES), jnp.float32),
            pltpu.VMEM(shape, jnp.float32),
            pltpu.SemaphoreType.DMA((4,)),
        ],
        compiler_params=pltpu.CompilerParams(vmem_limit_bytes=32 * 2**20),
        cost_estimate=pl.CostEstimate(flops=10**9, bytes_accessed=2**20, transcendentals=0),
        name="near_out",
    )(kept, taken)


def finish_kernel(far_ref, _, out_hbm, wide_ref, block_ref, sems, *, rows, chans):
    level = lax.axis_index("row") // 2
    col = lax.axis_index("col")
    per_row = 2 * chans
    half = rows // 2
    size = 3 * chans * SUB
    levels, bands, parts = block_ref.shape[:3]

    def widen(piece, of_half, count):
        for r in range(rows):
            for t in range(TILES):
                for s in range(2):
                    side = col if s == 0 else 1 - col
                    vals = far_ref[r * TILES + t, s * size + of_half : s * size + of_half + count, :]
                    vals = vals.astype(jnp.float32)
                    each = count // parts
                    for q in range(parts):
                        for k in range(chans):
                            to = (q * SUB + t * per_row + side * chans + k) * SUB
                            if each == SUB:
                                part = vals[q * SUB : (q + 1) * SUB]
                                part = part if k == 0 else pltpu.roll(part, SUB // 2, 0)
                            else:
                                part = vals[q * each + k * SUB : q * each + (k + 1) * SUB]
                            wide_ref[piece, r, pl.ds(pl.multiple_of(to, SUB), SUB), :] = part

    def copies(z):
        firsts = pl.ds(z * per_row, per_row)
        return [
            pltpu.make_async_copy(
                block_ref.at[z, b, q], out_hbm.at[b, q, firsts], sems.at[z, b * parts + q]
            )
            for b in range(bands)
            for q in range(parts)
        ]

    def send(z):
        piece, at = (z * per_row) // SUB, (z * per_row) % SUB
        for r in range(rows):
            for q in range(parts):
                for i in range(per_row):
                    spot = pl.ds(q * SUB * SUB + at + i, SUB, stride=SUB)
                    block_ref[z, r // half, q, i, r % half] = wide_ref[piece, r, spot, :]
        for copy in copies(z):
            copy.start()

    def wait(z):
        for copy in copies(z):
            copy.wait()

    def first_level():
        widen(0, 0, 2 * chans * SUB)
        send(0)

    def third_level():
        widen(1, 2 * chans * SUB, chans * SUB)
        send(2)

    pl.when(level > 0)(first_level)
    pl.when(level > 1)(lambda: send(1))
    pl.when(level > 2)(third_level)
    for z in range(levels):
        pl.when(level > z)(functools.partial(wait, z))


def finish_packed(far, out, rows, chans):
    hbm = pl.BlockSpec(memory_space=pltpu.HBM)
    levels, quads = rows // 2 - 1, out.shape[3]
    return pl.pallas_call(
        functools.partial(finish_kernel, rows=rows, chans=chans),
        out_shape=jax.ShapeDtypeStruct(out.shape, out.dtype),
        in_specs=[pl.BlockSpec(memory_space=pltpu.VMEM), hbm],
        out_specs=hbm,
        scratch_shapes=[
            pltpu.VMEM((2, rows, 2 * SUB * SUB, LANES), jnp.float32),
            pltpu.VMEM((levels, 2, 2, 2 * chans, quads, SUB, LANES), jnp.float32),
            pltpu.SemaphoreType.DMA((levels, 4)),
        ],
        input_output_aliases={1: 0},
        compiler_params=pltpu.CompilerParams(vmem_limit_bytes=32 * 2**20),
        cost_estimate=pl.CostEstimate(flops=10**9, bytes_accessed=2**20, transcendentals=0),
        name="finish",
    )(far, out)


def on_device_packed(spectra, window_flags):
    bands, windows, parts, chans, bins = spectra.shape
    rows, cols = lax.axis_size("row"), lax.axis_size("col")
    chunks = bins // LANES
    view = spectra.reshape(bands, windows, parts, chans, chunks, LANES)
    view = view.transpose(0, 1, 2, 4, 3, 5).reshape(bands, windows, parts, chunks * chans, LANES)

    def swap(value):
        return lax.ppermute(value, "col", [(0, 1), (1, 0)])

    own = whiten_packed(view, window_flags.T)
    got = lax.all_to_all(own, "row", 0, 0, tiled=True)

    def level_swap(value):
        return lax.ppermute(value, "row", [(r, r ^ 1) for r in range(rows)])

    keep, give = halves_packed(own)
    took = level_swap(give)
    keep_other = swap(keep)
    got, took, keep_other = lax.optimization_barrier((got, took, keep_other))
    far = far_packed(got, swap, rows, chans, windows)
    far = lax.all_to_all(far, "row", 0, 0, tiled=True)
    kept, give = near_packed(keep, keep_other, took, swap(took), windows)
    out = near_out_packed(kept, level_swap(give), rows, chans)
    out = finish_packed(far, out, rows, chans)
    out = out.reshape(bands, 2, rows * chans, chunks, cols * chans, LANES)
    out = out.transpose(0, 1, 2, 4, 3, 5)
    return out.reshape(bands, 2, 1, rows * chans, cols * chans, bins)


def on_device(spectra, window_flags):
    bands, windows, _, chans, bins = spectra.shape
    rows, cols = lax.axis_size("row"), lax.axis_size("col")
    if (
        bands == 2
        and rows == 8
        and bands * bins == rows * TILES * LANES
        and cols == 2
        and chans == 2
        and windows % 16 == 0
        and bins == rows * LANES
    ):
        return on_device_packed(spectra, window_flags)
    payload = whiten_plain(spectra, window_flags, rows * cols)
    got = lax.all_to_all(payload, ("row", "col"), 0, 0, tiled=True)
    result = cross_plain(got, rows, cols, chans, windows)
    back = lax.all_to_all(result, ("row", "col"), 0, 0, tiled=True)
    return finish_plain(back, bands, bins, rows, cols, chans)


def solution(mesh):
    in_specs = (P("parts", None, None, ("row", "col"), None), P("parts", ("row", "col")))
    out_specs = P("parts", None, "col", None, "row", None)
    return jax.shard_map(
        on_device, mesh=mesh, in_specs=in_specs, out_specs=out_specs, check_vma=False
    )
```

```python
import functools

import jax
import jax.numpy as jnp
from jax import lax
from jax.experimental import pallas as pl
from jax.experimental.pallas import tpu as pltpu
from jax.sharding import PartitionSpec as P

HALFWIN = 64
LANES = 128
SUB = 8

epsilon = 1e-06


def window_mean(magnitude):
    bins = magnitude.shape[-1]
    lead = [(0, 0)] * (magnitude.ndim - 1)
    padded = jnp.pad(magnitude, lead + [(HALFWIN + 1, HALFWIN)])
    running = jnp.cumsum(padded, axis=-1)
    total = running[..., 2 * HALFWIN + 1 :] - running[..., :bins]
    positions = jnp.arange(bins, dtype=jnp.int32)
    counted = (
        jnp.minimum(positions + HALFWIN, bins - 1) - jnp.maximum(positions - HALFWIN, 0) + 1
    ).astype(jnp.float32)
    return total / counted


def whiten_plain(spectra, window_flags, devices):
    bands, windows, parts, chans, bins = spectra.shape
    flags = window_flags.astype(jnp.float32)[None, :, None, :, None]
    values = spectra.astype(jnp.float32) * flags
    magnitude = jnp.sqrt(values[:, :, 0] * values[:, :, 0] + values[:, :, 1] * values[:, :, 1])
    smooth = window_mean(magnitude)
    white = (values / (smooth[:, :, None] + epsilon)).astype(jnp.bfloat16)
    own = bands * bins // devices
    white = white.reshape(bands, windows, parts, chans, bins // own, own)
    white = white.transpose(0, 4, 3, 2, 1, 5)
    return white.reshape(devices, chans * parts * windows, own)


def cross_plain(got, rows, cols, chans, windows):
    own = got.shape[-1]
    data = got.reshape(rows * cols * chans, 2, windows, own)
    prods = jnp.einsum("apwf,jqwf->pqajf", data, data, preferred_element_type=jnp.float32)
    both = jnp.stack([prods[0, 0] + prods[1, 1], prods[1, 0] - prods[0, 1]])
    both = both.reshape(2, rows, cols, chans, rows, cols * chans, own)
    both = both.transpose(4, 2, 0, 1, 3, 5, 6).astype(jnp.bfloat16)
    return both.reshape(rows * cols, 2 * rows * chans * cols * chans, own)


def finish_plain(got, bands, bins, rows, cols, chans):
    own = got.shape[-1]
    row, col = lax.axis_index("row"), lax.axis_index("col")
    data = got.reshape(bands, bins // own, 2, rows * chans, cols * chans, own)
    data = data.transpose(0, 2, 3, 4, 1, 5).reshape(
        bands, 2, rows * chans, cols * chans, bins
    )
    slot = jnp.arange(rows * chans, dtype=jnp.int32)
    first = (slot // chans * cols + col) * chans + slot % chans
    second = row * cols * chans + jnp.arange(cols * chans, dtype=jnp.int32)
    keep = (first[:, None] <= second[None, :])[:, :, None]
    return jnp.where(keep, data.astype(jnp.float32), 0.0)[:, :, None]


TILES = 2
VMEM_FIRST = 65454080


def whiten_kernel(
    flags_hbm, x_hbm, out_hbm, flags_ref, x_ref, white_ref, out_ref, sems, out_sems, *, chans
):
    bands, windows, _, group, _ = x_ref.shape
    chunks = group // chans
    step = 32
    steps = windows // step
    rows = step * group

    copies = [pltpu.make_async_copy(flags_hbm, flags_ref, sems.at[bands * steps])]
    for n in range(bands * steps):
        part = (n // steps, pl.ds(n % steps * step, step))
        copies.append(pltpu.make_async_copy(x_hbm.at[part], x_ref.at[part], sems.at[n]))
    for copy in copies:
        copy.start()

    row_id = lax.broadcasted_iota(jnp.int32, (rows, LANES), 0) % group
    lane_id = lax.broadcasted_iota(jnp.int32, (rows, LANES), 1)
    spot = row_id // chans * LANES + lane_id
    last = chunks * LANES - 1
    counted = jnp.minimum(spot + HALFWIN, last) - jnp.maximum(spot - HALFWIN, 0) + 1
    inv_count = 1.0 / counted.astype(jnp.float32)
    has_prev = row_id >= chans
    has_next = row_id < group - chans
    k_id = lax.broadcasted_iota(jnp.int32, (group, LANES), 0) % chans
    src = lax.broadcasted_iota(jnp.int32, (2 * LANES, 3 * LANES), 0) % LANES
    dst = lax.broadcasted_iota(jnp.int32, (2 * LANES, 3 * LANES), 1) - LANES
    band_mat = jnp.where(jnp.abs(src - dst) <= HALFWIN, 1.0, 0.0).astype(jnp.bfloat16)

    copies[0].wait()
    for b in range(bands):
        for n in range(steps):
            w0 = n * step
            copies[1 + b * steps + n].wait()
            x = x_ref[b, w0 : w0 + step].astype(jnp.float32)
            keeps = []
            for s in range(step):
                keep = jnp.full((group, LANES), flags_ref[0, w0 + s], jnp.int32)
                for k in range(1, chans):
                    keep = jnp.where(k_id == k, flags_ref[k, w0 + s], keep)
                keeps.append(keep)
            keep = jnp.stack(keeps).astype(jnp.float32)
            re = (x[:, 0] * keep).reshape(rows, LANES)
            im = (x[:, 1] * keep).reshape(rows, LANES)
            mag = jnp.sqrt(re * re + im * im)
            high = mag.astype(jnp.bfloat16)
            rest = (mag - high.astype(jnp.float32)).astype(jnp.bfloat16)
            both = jnp.concatenate([high, rest], axis=1)
            sums = jnp.dot(both, band_mat, preferred_element_type=jnp.float32)
            total = sums[:, LANES : 2 * LANES]
            total += jnp.where(has_prev, pltpu.roll(sums[:, 2 * LANES :], chans, 0), 0.0)
            total += jnp.where(has_next, pltpu.roll(sums[:, :LANES], rows - chans, 0), 0.0)
            inv = 1.0 / (total * inv_count + epsilon)
            for p, part in enumerate((re, im)):
                start = ((b * 2 + p) * windows + w0) * group
                white_ref[start : start + rows, :] = part * inv
        for c in range(chunks):
            for k in range(chans):
                for p in range(2):
                    start = (b * 2 + p) * windows * group + c * chans + k
                    slab = white_ref[pl.ds(start, windows, stride=group), :]
                    at = (k * 2 + p) * windows
                    out_ref[b * chunks + c, at : at + windows, :] = slab.astype(jnp.bfloat16)
            if c % TILES == TILES - 1:
                n = (b * chunks + c) // TILES
                part = pl.ds(n * TILES, TILES)
                copy = pltpu.make_async_copy(out_ref.at[part], out_hbm.at[part], out_sems.at[n])
                copy.start()
                copies.append(copy)
    for copy in copies[1 + bands * steps :]:
        copy.wait()


def whiten_packed(view, flags):
    bands, windows, parts, group, _ = view.shape
    chans = flags.shape[0]
    tiles = bands * group // chans
    hbm = pl.BlockSpec(memory_space=pltpu.HBM)
    shape = (tiles, chans * parts * windows, LANES)
    return pl.pallas_call(
        functools.partial(whiten_kernel, chans=chans),
        out_shape=jax.ShapeDtypeStruct(shape, jnp.bfloat16),
        in_specs=[hbm, hbm],
        out_specs=hbm,
        scratch_shapes=[
            pltpu.SMEM(flags.shape, jnp.int32),
            pltpu.VMEM(view.shape, jnp.bfloat16),
            pltpu.VMEM((bands * parts * windows * group, LANES), jnp.float32),
            pltpu.VMEM(shape, jnp.bfloat16),
            pltpu.SemaphoreType.DMA((bands * windows // 16 + 1,)),
            pltpu.SemaphoreType.DMA((tiles // TILES,)),
        ],
        compiler_params=pltpu.CompilerParams(vmem_limit_bytes=VMEM_FIRST),
        cost_estimate=pl.CostEstimate(flops=10**9, bytes_accessed=2**20, transcendentals=0),
        name="whiten",
    )(flags, view)


def spread_second(second_ref, values, windows, chans):
    for k in range(chans):
        row = k * 2 * windows
        re = values[row : row + windows].astype(jnp.float32)
        im = values[row + windows : row + 2 * windows].astype(jnp.float32)
        second_ref[k, 0] = re
        second_ref[k, 1] = im - re
        second_ref[k, 2] = re + im


def spread_first(first_ref, row_at, values, windows, chans):
    for k in range(chans):
        row = k * 2 * windows
        re = values[row : row + windows].astype(jnp.float32)
        im = values[row + windows : row + 2 * windows].astype(jnp.float32)
        slot = pl.ds(row_at * chans + k, windows, stride=SUB)
        first_ref[0, slot, :] = re + im
        first_ref[1, slot, :] = im
        first_ref[2, slot, :] = re


def pair_sums(work, windows):
    zero = jnp.zeros((SUB, LANES), jnp.float32)

    def body(w, sums):
        base = pl.multiple_of(w * SUB, SUB)
        loaded = {}

        def load(ref, at):
            if id(ref) not in loaded:
                loaded[id(ref)] = [ref[q, at, :] for q in range(3)]
            return loaded[id(ref)]

        out = []
        for (first_ref, second_ref), (s1, s2, s3) in zip(work, sums):
            f = load(first_ref, pl.ds(base, SUB))
            g = load(second_ref, pl.ds(w, 1))
            out.append((s1 + g[0] * f[0], s2 + g[1] * f[1], s3 + g[2] * f[2]))
        return tuple(out)

    sums = lax.fori_loop(0, windows, body, ((zero, zero, zero),) * len(work), unroll=32)
    return [(s1 + s2, s1 - s3) for s1, s2, s3 in sums]


def far_sums(first_ref, values_ref, second_ref, put, rows, chans, windows, done=None):
    low = lax.broadcasted_iota(jnp.int32, (SUB, LANES), 0) < SUB // 2
    for t in range(TILES):
        firsts = [first_ref.at[block, t] for block in range(2)]
        seconds = {}
        for r in range(2, rows):
            spread_second(second_ref.at[t, r], values_ref[r * TILES + t], windows, chans)
            seconds[r] = [second_ref.at[t, r, k] for k in range(chans)]
        mid = range(2, rows - 2)
        sums = pair_sums([(firsts[0], g) for r in mid for g in seconds[r]], windows)
        for n, r in enumerate(mid):
            for q in range(2):
                vals = jnp.concatenate([sums[n * chans + k][q] for k in range(chans)])
                put(r, t, q * chans * SUB, vals)
        if done is not None:
            done(mid, t)
        last = range(rows - 2, rows)
        sums = pair_sums([(f, g) for r in last for g in seconds[r] for f in firsts], windows)
        for n, r in enumerate(last):
            mine = sums[n * 2 * chans : (n + 1) * 2 * chans]
            rest = []
            for q in range(2):
                vals = jnp.concatenate([mine[k * 2][q] for k in range(chans)])
                put(r, t, q * chans * SUB, vals)
                rest.append(jnp.where(low, mine[1][q], pltpu.roll(mine[3][q], SUB // 2, 0)))
            put(r, t, 2 * chans * SUB, jnp.concatenate(rest))
        if done is not None:
            done(last, t)


def far_own_kernel(got_ref, first_ref, out_ref, second_ref, *, rows, chans, windows):
    for t in range(TILES):
        for r in range(rows - 2):
            spread_first(
                first_ref.at[r * chans // SUB, t],
                r % (SUB // chans),
                got_ref[r * TILES + t],
                windows,
                chans,
            )

    def put(r, t, at, vals):
        out_ref[r * TILES + t, at : at + 2 * SUB, :] = vals.astype(jnp.bfloat16)

    far_sums(first_ref, got_ref, second_ref, put, rows, chans, windows)


def far_other_kernel(
    other_ref, first_ref, own_ref, out_hbm, second_ref, out_ref, sems, *, rows, chans, windows
):
    size = own_ref.shape[1]
    copies = []

    def send(first, count):
        part = pl.ds(first, count)
        sem = sems.at[len(copies)]
        copies.append(pltpu.make_async_copy(out_ref.at[part], out_hbm.at[part], sem))
        copies[-1].start()

    out_ref[: 2 * TILES] = jnp.zeros((2 * TILES, *out_ref.shape[1:]), out_ref.dtype)
    send(0, 2 * TILES)
    mid = pl.ds(2 * TILES, (rows - 4) * TILES)
    rest = jnp.zeros(((rows - 4) * TILES, 2 * SUB, LANES), out_ref.dtype)
    out_ref[2 * TILES :, :size, :] = own_ref[2 * TILES :]
    for s in range(2):
        out_ref[mid, s * size + 4 * SUB : s * size + 6 * SUB, :] = rest

    def put(r, t, at, vals):
        at += size
        out_ref[r * TILES + t, at : at + 2 * SUB, :] = vals.astype(jnp.bfloat16)

    def done(which, t):
        for r in which:
            send(r * TILES + t, 1)

    far_sums(first_ref, other_ref, second_ref, put, rows, chans, windows, done)
    for copy in copies:
        copy.wait()


def far_packed(got, swap, rows, chans, windows):
    vmem = pl.BlockSpec(memory_space=pltpu.VMEM)
    scratch = [pltpu.VMEM((TILES, rows, chans, 3, windows, LANES), jnp.float32)]
    params = dict(
        compiler_params=pltpu.CompilerParams(vmem_limit_bytes=32 * 2**20),
        cost_estimate=pl.CostEstimate(flops=10**9, bytes_accessed=2**20, transcendentals=0),
    )
    size = 3 * chans * SUB
    sizes = dict(rows=rows, chans=chans, windows=windows)
    first, own = pl.pallas_call(
        functools.partial(far_own_kernel, **sizes),
        out_shape=[
            jax.ShapeDtypeStruct((2, TILES, 3, windows * SUB, LANES), jnp.float32),
            jax.ShapeDtypeStruct((rows * TILES, size, LANES), jnp.bfloat16),
        ],
        in_specs=[vmem],
        out_specs=[vmem] * 2,
        scratch_shapes=scratch,
        name="far_own",
        **params,
    )(got)
    return pl.pallas_call(
        functools.partial(far_other_kernel, **sizes),
        out_shape=jax.ShapeDtypeStruct((rows * TILES, 2 * size, LANES), jnp.bfloat16),
        in_specs=[vmem] * 3,
        out_specs=pl.BlockSpec(memory_space=pltpu.HBM),
        scratch_shapes=scratch
        + [
            pltpu.VMEM((rows * TILES, 2 * size, LANES), jnp.bfloat16),
            pltpu.SemaphoreType.DMA((1 + (rows - 2) * TILES,)),
        ],
        name="far_other",
        **params,
    )(swap(got), first, own)


def halves_kernel(own_ref, keep_ref, give_ref):
    odd = lax.axis_index("row") % 2
    tiles = keep_ref.shape[0]
    keep_ref[...] = own_ref[pl.ds(odd * tiles, tiles)]
    give_ref[...] = own_ref[pl.ds((1 - odd) * tiles, tiles)]


def halves_packed(own):
    vmem = pl.BlockSpec(memory_space=pltpu.VMEM)
    band = jax.ShapeDtypeStruct((own.shape[0] // 2, *own.shape[1:]), own.dtype)
    return pl.pallas_call(
        halves_kernel,
        out_shape=[band] * 2,
        in_specs=[vmem],
        out_specs=[vmem] * 2,
        compiler_params=pltpu.CompilerParams(vmem_limit_bytes=32 * 2**20),
        cost_estimate=pl.CostEstimate(flops=10**9, bytes_accessed=2**20, transcendentals=0),
        name="halves",
    )(own)


def near_kernel(*refs, windows):
    sources, outs, (first_ref, second_ref) = refs[:4], refs[4:6], refs[6:]
    chans = 2
    odd = lax.axis_index("row") % 2
    low = lax.broadcasted_iota(jnp.int32, (SUB, LANES), 0) < SUB // 2
    tiles = outs[0].shape[0]

    def body(m, carry):
        for t in range(TILES):
            tile = m * TILES + t
            first = first_ref.at[t]
            work = []
            for n in range(2):
                own_ref, other_ref = sources[2 * n : 2 * n + 2]
                spread_first(first, odd if n == 0 else 1 - odd, own_ref[tile], windows, chans)
                for s, ref in enumerate((own_ref, other_ref)):
                    spread_second(second_ref.at[t, n, s], ref[tile], windows, chans)
                    work += [(first, second_ref.at[t, n, s, k]) for k in range(chans)]
            sums = pair_sums(work, windows)
            for n, out_ref in enumerate(outs):
                for s in range(2):
                    one, two = sums[(n * 2 + s) * chans : (n * 2 + s + 1) * chans]
                    vals = [
                        jnp.where(low, one[q], pltpu.roll(two[q], SUB // 2, 0)) for q in range(2)
                    ]
                    vals = jnp.concatenate(vals).astype(jnp.bfloat16)
                    out_ref[tile, s * 2 * SUB : (s + 1) * 2 * SUB, :] = vals
        return carry

    lax.fori_loop(0, tiles // TILES, body, 0)


def near_packed(keep, keep_other, took, took_other, windows):
    vmem = pl.BlockSpec(memory_space=pltpu.VMEM)
    piece = jax.ShapeDtypeStruct((keep.shape[0], 4 * SUB, LANES), jnp.bfloat16)
    return pl.pallas_call(
        functools.partial(near_kernel, windows=windows),
        out_shape=[piece] * 2,
        in_specs=[vmem] * 4,
        out_specs=[vmem] * 2,
        scratch_shapes=[
            pltpu.VMEM((TILES, 3, windows * SUB, LANES), jnp.float32),
            pltpu.VMEM((TILES, 2, 2, 2, 3, windows, LANES), jnp.float32),
        ],
        compiler_params=pltpu.CompilerParams(vmem_limit_bytes=32 * 2**20),
        cost_estimate=pl.CostEstimate(flops=10**9, bytes_accessed=2**20, transcendentals=0),
        name="near",
    )(keep, keep_other, took, took_other)


def near_out_kernel(kept_ref, taken_ref, out_hbm, wide_ref, out_ref, sems, *, chans):
    level, odd = lax.axis_index("row") // 2, lax.axis_index("row") % 2
    col = lax.axis_index("col")
    per_row = 2 * chans
    bands, parts, _, quads, _, _ = out_ref.shape
    second = odd * per_row + lax.broadcasted_iota(jnp.int32, (SUB, LANES), 0) % per_row
    for n, ref in enumerate((kept_ref, taken_ref)):
        for m in range(quads):
            for t in range(TILES):
                for s in range(2):
                    side = col if s == 0 else 1 - col
                    vals = ref[m * TILES + t, s * 2 * SUB : (s + 1) * 2 * SUB, :]
                    vals = vals.astype(jnp.float32)
                    for q in range(parts):
                        for k in range(chans):
                            to = (q * SUB + t * per_row + side * chans + k) * SUB
                            part = vals[q * SUB : (q + 1) * SUB]
                            part = part if k == 0 else pltpu.roll(part, SUB // 2, 0)
                            wide_ref[n, m, pl.ds(pl.multiple_of(to, SUB), SUB), :] = part
    copies = []
    for b in range(bands):
        for q in range(parts):
            out_ref[b, q] = jnp.zeros(out_ref.shape[2:], out_ref.dtype)
            for m in range(quads):
                for i in range(per_row):
                    first = i // chans * per_row + col * chans + i % chans
                    spot = pl.ds(q * SUB * SUB + i, SUB, stride=SUB)
                    vals = wide_ref[b ^ odd, m, spot, :]
                    out_ref[b, q, level * per_row + i, m] = jnp.where(first <= second, vals, 0.0)
            sem = sems.at[b * parts + q]
            copies.append(pltpu.make_async_copy(out_ref.at[b, q], out_hbm.at[b, q], sem))
            copies[-1].start()
    for copy in copies:
        copy.wait()


def near_out_packed(kept, taken, rows, chans):
    vmem = pl.BlockSpec(memory_space=pltpu.VMEM)
    shape = (2, 2, rows * chans, rows // 2, SUB, LANES)
    return pl.pallas_call(
        functools.partial(near_out_kernel, chans=chans),
        out_shape=jax.ShapeDtypeStruct(shape, jnp.float32),
        in_specs=[vmem] * 2,
        out_specs=pl.BlockSpec(memory_space=pltpu.HBM),
        scratch_shapes=[
            pltpu.VMEM((2, rows // 2, 2 * SUB * SUB, LANES), jnp.float32),
            pltpu.VMEM(shape, jnp.float32),
            pltpu.SemaphoreType.DMA((4,)),
        ],
        compiler_params=pltpu.CompilerParams(vmem_limit_bytes=32 * 2**20),
        cost_estimate=pl.CostEstimate(flops=10**9, bytes_accessed=2**20, transcendentals=0),
        name="near_out",
    )(kept, taken)


def finish_kernel(far_ref, _, out_hbm, wide_ref, block_ref, sems, *, rows, chans):
    level = lax.axis_index("row") // 2
    col = lax.axis_index("col")
    per_row = 2 * chans
    half = rows // 2
    size = 3 * chans * SUB
    levels, bands, parts = block_ref.shape[:3]

    def widen(piece, of_half, count):
        for r in range(rows):
            for t in range(TILES):
                for s in range(2):
                    side = col if s == 0 else 1 - col
                    vals = far_ref[r * TILES + t, s * size + of_half : s * size + of_half + count, :]
                    vals = vals.astype(jnp.float32)
                    each = count // parts
                    for q in range(parts):
                        for k in range(chans):
                            to = (q * SUB + t * per_row + side * chans + k) * SUB
                            if each == SUB:
                                part = vals[q * SUB : (q + 1) * SUB]
                                part = part if k == 0 else pltpu.roll(part, SUB // 2, 0)
                            else:
                                part = vals[q * each + k * SUB : q * each + (k + 1) * SUB]
                            wide_ref[piece, r, pl.ds(pl.multiple_of(to, SUB), SUB), :] = part

    def copies(z):
        firsts = pl.ds(z * per_row, per_row)
        return [
            pltpu.make_async_copy(
                block_ref.at[z, b, q], out_hbm.at[b, q, firsts], sems.at[z, b * parts + q]
            )
            for b in range(bands)
            for q in range(parts)
        ]

    def send(z):
        piece, at = (z * per_row) // SUB, (z * per_row) % SUB
        for r in range(rows):
            for q in range(parts):
                for i in range(per_row):
                    spot = pl.ds(q * SUB * SUB + at + i, SUB, stride=SUB)
                    block_ref[z, r // half, q, i, r % half] = wide_ref[piece, r, spot, :]
        for copy in copies(z):
            copy.start()

    def wait(z):
        for copy in copies(z):
            copy.wait()

    def first_level():
        widen(0, 0, 2 * chans * SUB)
        send(0)

    def third_level():
        widen(1, 2 * chans * SUB, chans * SUB)
        send(2)

    pl.when(level > 0)(first_level)
    pl.when(level > 1)(lambda: send(1))
    pl.when(level > 2)(third_level)
    for z in range(levels):
        pl.when(level > z)(functools.partial(wait, z))


def finish_packed(far, out, rows, chans):
    hbm = pl.BlockSpec(memory_space=pltpu.HBM)
    levels, quads = rows // 2 - 1, out.shape[3]
    return pl.pallas_call(
        functools.partial(finish_kernel, rows=rows, chans=chans),
        out_shape=jax.ShapeDtypeStruct(out.shape, out.dtype),
        in_specs=[pl.BlockSpec(memory_space=pltpu.VMEM), hbm],
        out_specs=hbm,
        scratch_shapes=[
            pltpu.VMEM((2, rows, 2 * SUB * SUB, LANES), jnp.float32),
            pltpu.VMEM((levels, 2, 2, 2 * chans, quads, SUB, LANES), jnp.float32),
            pltpu.SemaphoreType.DMA((levels, 4)),
        ],
        input_output_aliases={1: 0},
        compiler_params=pltpu.CompilerParams(vmem_limit_bytes=32 * 2**20),
        cost_estimate=pl.CostEstimate(flops=10**9, bytes_accessed=2**20, transcendentals=0),
        name="finish",
    )(far, out)


def on_device_packed(spectra, window_flags):
    bands, windows, parts, chans, bins = spectra.shape
    rows, cols = lax.axis_size("row"), lax.axis_size("col")
    chunks = bins // LANES
    view = spectra.reshape(bands, windows, parts, chans, chunks, LANES)
    view = view.transpose(0, 1, 2, 4, 3, 5).reshape(bands, windows, parts, chunks * chans, LANES)

    def swap(value):
        return lax.ppermute(value, "col", [(0, 1), (1, 0)])

    own = whiten_packed(view, window_flags.T)
    got = lax.all_to_all(own, "row", 0, 0, tiled=True)

    def level_swap(value):
        return lax.ppermute(value, "row", [(r, r ^ 1) for r in range(rows)])

    keep, give = halves_packed(own)
    took = level_swap(give)
    keep_other = swap(keep)
    got, took, keep_other = lax.optimization_barrier((got, took, keep_other))
    far = far_packed(got, swap, rows, chans, windows)
    far = lax.all_to_all(far, "row", 0, 0, tiled=True)
    kept, give = near_packed(keep, keep_other, took, swap(took), windows)
    out = near_out_packed(kept, level_swap(give), rows, chans)
    out = finish_packed(far, out, rows, chans)
    out = out.reshape(bands, 2, rows * chans, chunks, cols * chans, LANES)
    out = out.transpose(0, 1, 2, 4, 3, 5)
    return out.reshape(bands, 2, 1, rows * chans, cols * chans, bins)


def on_device(spectra, window_flags):
    bands, windows, _, chans, bins = spectra.shape
    rows, cols = lax.axis_size("row"), lax.axis_size("col")
    if (
        bands == 2
        and rows == 8
        and bands * bins == rows * TILES * LANES
        and cols == 2
        and chans == 2
        and windows % 16 == 0
        and bins == rows * LANES
    ):
        return on_device_packed(spectra, window_flags)
    payload = whiten_plain(spectra, window_flags, rows * cols)
    got = lax.all_to_all(payload, ("row", "col"), 0, 0, tiled=True)
    result = cross_plain(got, rows, cols, chans, windows)
    back = lax.all_to_all(result, ("row", "col"), 0, 0, tiled=True)
    return finish_plain(back, bands, bins, rows, cols, chans)


def solution(mesh):
    in_specs = (P("parts", None, None, ("row", "col"), None), P("parts", ("row", "col")))
    out_specs = P("parts", None, "col", None, "row", None)
    return jax.shard_map(
        on_device, mesh=mesh, in_specs=in_specs, out_specs=out_specs, check_vma=False
    )
```

```python
import functools

import jax
import jax.numpy as jnp
from jax import lax
from jax.experimental import pallas as pl
from jax.experimental.pallas import tpu as pltpu
from jax.sharding import PartitionSpec as P

HALFWIN = 64
LANES = 128
SUB = 8

epsilon = 1e-06


def window_mean(magnitude):
    bins = magnitude.shape[-1]
    lead = [(0, 0)] * (magnitude.ndim - 1)
    padded = jnp.pad(magnitude, lead + [(HALFWIN + 1, HALFWIN)])
    running = jnp.cumsum(padded, axis=-1)
    total = running[..., 2 * HALFWIN + 1 :] - running[..., :bins]
    positions = jnp.arange(bins, dtype=jnp.int32)
    counted = (
        jnp.minimum(positions + HALFWIN, bins - 1) - jnp.maximum(positions - HALFWIN, 0) + 1
    ).astype(jnp.float32)
    return total / counted


def whiten_plain(spectra, window_flags, devices):
    bands, windows, parts, chans, bins = spectra.shape
    flags = window_flags.astype(jnp.float32)[None, :, None, :, None]
    values = spectra.astype(jnp.float32) * flags
    magnitude = jnp.sqrt(values[:, :, 0] * values[:, :, 0] + values[:, :, 1] * values[:, :, 1])
    smooth = window_mean(magnitude)
    white = (values / (smooth[:, :, None] + epsilon)).astype(jnp.bfloat16)
    own = bands * bins // devices
    white = white.reshape(bands, windows, parts, chans, bins // own, own)
    white = white.transpose(0, 4, 3, 2, 1, 5)
    return white.reshape(devices, chans * parts * windows, own)


def cross_plain(got, rows, cols, chans, windows):
    own = got.shape[-1]
    data = got.reshape(rows * cols * chans, 2, windows, own)
    prods = jnp.einsum("apwf,jqwf->pqajf", data, data, preferred_element_type=jnp.float32)
    both = jnp.stack([prods[0, 0] + prods[1, 1], prods[1, 0] - prods[0, 1]])
    both = both.reshape(2, rows, cols, chans, rows, cols * chans, own)
    both = both.transpose(4, 2, 0, 1, 3, 5, 6).astype(jnp.bfloat16)
    return both.reshape(rows * cols, 2 * rows * chans * cols * chans, own)


def finish_plain(got, bands, bins, rows, cols, chans):
    own = got.shape[-1]
    row, col = lax.axis_index("row"), lax.axis_index("col")
    data = got.reshape(bands, bins // own, 2, rows * chans, cols * chans, own)
    data = data.transpose(0, 2, 3, 4, 1, 5).reshape(
        bands, 2, rows * chans, cols * chans, bins
    )
    slot = jnp.arange(rows * chans, dtype=jnp.int32)
    first = (slot // chans * cols + col) * chans + slot % chans
    second = row * cols * chans + jnp.arange(cols * chans, dtype=jnp.int32)
    keep = (first[:, None] <= second[None, :])[:, :, None]
    return jnp.where(keep, data.astype(jnp.float32), 0.0)[:, :, None]


TILES = 2
VMEM_FIRST = 65454080


def whiten_kernel(
    flags_hbm, x_hbm, out_hbm, flags_ref, x_ref, white_ref, out_ref, sems, out_sems, *, chans
):
    bands, windows, _, group, _ = x_ref.shape
    chunks = group // chans
    step = 32
    steps = windows // step
    rows = step * group

    copies = [pltpu.make_async_copy(flags_hbm, flags_ref, sems.at[bands * steps])]
    for n in range(bands * steps):
        part = (n // steps, pl.ds(n % steps * step, step))
        copies.append(pltpu.make_async_copy(x_hbm.at[part], x_ref.at[part], sems.at[n]))
    for copy in copies:
        copy.start()

    row_id = lax.broadcasted_iota(jnp.int32, (rows, LANES), 0) % group
    lane_id = lax.broadcasted_iota(jnp.int32, (rows, LANES), 1)
    spot = row_id // chans * LANES + lane_id
    last = chunks * LANES - 1
    counted = jnp.minimum(spot + HALFWIN, last) - jnp.maximum(spot - HALFWIN, 0) + 1
    inv_count = 1.0 / counted.astype(jnp.float32)
    has_prev = row_id >= chans
    has_next = row_id < group - chans
    k_id = lax.broadcasted_iota(jnp.int32, (group, LANES), 0) % chans
    src = lax.broadcasted_iota(jnp.int32, (2 * LANES, 3 * LANES), 0) % LANES
    dst = lax.broadcasted_iota(jnp.int32, (2 * LANES, 3 * LANES), 1) - LANES
    band_mat = jnp.where(jnp.abs(src - dst) <= HALFWIN, 1.0, 0.0).astype(jnp.bfloat16)

    for copy in copies:
        copy.wait()
    for b in range(bands):
        for n in range(steps):
            w0 = n * step
            x = x_ref[b, w0 : w0 + step].astype(jnp.float32)
            keeps = []
            for s in range(step):
                keep = jnp.full((group, LANES), flags_ref[0, w0 + s], jnp.int32)
                for k in range(1, chans):
                    keep = jnp.where(k_id == k, flags_ref[k, w0 + s], keep)
                keeps.append(keep)
            keep = jnp.stack(keeps).astype(jnp.float32)
            re = (x[:, 0] * keep).reshape(rows, LANES)
            im = (x[:, 1] * keep).reshape(rows, LANES)
            mag = jnp.sqrt(re * re + im * im)
            high = mag.astype(jnp.bfloat16)
            rest = (mag - high.astype(jnp.float32)).astype(jnp.bfloat16)
            both = jnp.concatenate([high, rest], axis=1)
            sums = jnp.dot(both, band_mat, preferred_element_type=jnp.float32)
            total = sums[:, LANES : 2 * LANES]
            total += jnp.where(has_prev, pltpu.roll(sums[:, 2 * LANES :], chans, 0), 0.0)
            total += jnp.where(has_next, pltpu.roll(sums[:, :LANES], rows - chans, 0), 0.0)
            inv = 1.0 / (total * inv_count + epsilon)
            for p, part in enumerate((re, im)):
                start = ((b * 2 + p) * windows + w0) * group
                white_ref[start : start + rows, :] = part * inv
        for c in range(chunks):
            for k in range(chans):
                for p in range(2):
                    start = (b * 2 + p) * windows * group + c * chans + k
                    slab = white_ref[pl.ds(start, windows, stride=group), :]
                    at = (k * 2 + p) * windows
                    out_ref[b * chunks + c, at : at + windows, :] = slab.astype(jnp.bfloat16)
            if c % TILES == TILES - 1:
                n = (b * chunks + c) // TILES
                part = pl.ds(n * TILES, TILES)
                copy = pltpu.make_async_copy(out_ref.at[part], out_hbm.at[part], out_sems.at[n])
                copy.start()
                copies.append(copy)
    for copy in copies[1 + bands * steps :]:
        copy.wait()


def whiten_packed(view, flags):
    bands, windows, parts, group, _ = view.shape
    chans = flags.shape[0]
    tiles = bands * group // chans
    hbm = pl.BlockSpec(memory_space=pltpu.HBM)
    shape = (tiles, chans * parts * windows, LANES)
    return pl.pallas_call(
        functools.partial(whiten_kernel, chans=chans),
        out_shape=jax.ShapeDtypeStruct(shape, jnp.bfloat16),
        in_specs=[hbm, hbm],
        out_specs=hbm,
        scratch_shapes=[
            pltpu.SMEM(flags.shape, jnp.int32),
            pltpu.VMEM(view.shape, jnp.bfloat16),
            pltpu.VMEM((bands * parts * windows * group, LANES), jnp.float32),
            pltpu.VMEM(shape, jnp.bfloat16),
            pltpu.SemaphoreType.DMA((bands * windows // 32 + 1,)),
            pltpu.SemaphoreType.DMA((tiles // TILES,)),
        ],
        compiler_params=pltpu.CompilerParams(vmem_limit_bytes=VMEM_FIRST),
        cost_estimate=pl.CostEstimate(flops=10**9, bytes_accessed=2**20, transcendentals=0),
        name="whiten",
    )(flags, view)


def spread_second(second_ref, values, windows, chans):
    for k in range(chans):
        row = k * 2 * windows
        re = values[row : row + windows].astype(jnp.float32)
        im = values[row + windows : row + 2 * windows].astype(jnp.float32)
        second_ref[k, 0] = re
        second_ref[k, 1] = im - re
        second_ref[k, 2] = re + im


def spread_first(first_ref, row_at, values, windows, chans):
    for k in range(chans):
        row = k * 2 * windows
        re = values[row : row + windows].astype(jnp.float32)
        im = values[row + windows : row + 2 * windows].astype(jnp.float32)
        slot = pl.ds(row_at * chans + k, windows, stride=SUB)
        first_ref[0, slot, :] = re + im
        first_ref[1, slot, :] = im
        first_ref[2, slot, :] = re


def pair_sums(work, windows):
    zero = jnp.zeros((SUB, LANES), jnp.float32)

    def body(w, sums):
        base = pl.multiple_of(w * SUB, SUB)
        loaded = {}

        def load(ref, at):
            if id(ref) not in loaded:
                loaded[id(ref)] = [ref[q, at, :] for q in range(3)]
            return loaded[id(ref)]

        out = []
        for (first_ref, second_ref), (s1, s2, s3) in zip(work, sums):
            f = load(first_ref, pl.ds(base, SUB))
            g = load(second_ref, pl.ds(w, 1))
            out.append((s1 + g[0] * f[0], s2 + g[1] * f[1], s3 + g[2] * f[2]))
        return tuple(out)

    sums = lax.fori_loop(0, windows, body, ((zero, zero, zero),) * len(work), unroll=32)
    return [(s1 + s2, s1 - s3) for s1, s2, s3 in sums]


def far_sums(first_ref, values_ref, second_ref, put, rows, chans, windows, done=None):
    low = lax.broadcasted_iota(jnp.int32, (SUB, LANES), 0) < SUB // 2
    for t in range(TILES):
        firsts = [first_ref.at[block, t] for block in range(2)]
        seconds = {}
        for r in range(2, rows):
            spread_second(second_ref.at[t, r], values_ref[r * TILES + t], windows, chans)
            seconds[r] = [second_ref.at[t, r, k] for k in range(chans)]
        mid = range(2, rows - 2)
        sums = pair_sums([(firsts[0], g) for r in mid for g in seconds[r]], windows)
        for n, r in enumerate(mid):
            for q in range(2):
                vals = jnp.concatenate([sums[n * chans + k][q] for k in range(chans)])
                put(r, t, q * chans * SUB, vals)
        if done is not None:
            done(mid, t)
        last = range(rows - 2, rows)
        sums = pair_sums([(f, g) for r in last for g in seconds[r] for f in firsts], windows)
        for n, r in enumerate(last):
            mine = sums[n * 2 * chans : (n + 1) * 2 * chans]
            rest = []
            for q in range(2):
                vals = jnp.concatenate([mine[k * 2][q] for k in range(chans)])
                put(r, t, q * chans * SUB, vals)
                rest.append(jnp.where(low, mine[1][q], pltpu.roll(mine[3][q], SUB // 2, 0)))
            put(r, t, 2 * chans * SUB, jnp.concatenate(rest))
        if done is not None:
            done(last, t)


def far_own_kernel(got_ref, first_ref, out_ref, second_ref, *, rows, chans, windows):
    for t in range(TILES):
        for r in range(rows - 2):
            spread_first(
                first_ref.at[r * chans // SUB, t],
                r % (SUB // chans),
                got_ref[r * TILES + t],
                windows,
                chans,
            )

    def put(r, t, at, vals):
        out_ref[r * TILES + t, at : at + 2 * SUB, :] = vals.astype(jnp.bfloat16)

    far_sums(first_ref, got_ref, second_ref, put, rows, chans, windows)


def far_other_kernel(
    other_ref, first_ref, own_ref, out_hbm, second_ref, out_ref, sems, *, rows, chans, windows
):
    size = own_ref.shape[1]
    copies = []

    def send(first, count):
        part = pl.ds(first, count)
        sem = sems.at[len(copies)]
        copies.append(pltpu.make_async_copy(out_ref.at[part], out_hbm.at[part], sem))
        copies[-1].start()

    out_ref[: 2 * TILES] = jnp.zeros((2 * TILES, *out_ref.shape[1:]), out_ref.dtype)
    send(0, 2 * TILES)
    mid = pl.ds(2 * TILES, (rows - 4) * TILES)
    rest = jnp.zeros(((rows - 4) * TILES, 2 * SUB, LANES), out_ref.dtype)
    out_ref[2 * TILES :, :size, :] = own_ref[2 * TILES :]
    for s in range(2):
        out_ref[mid, s * size + 4 * SUB : s * size + 6 * SUB, :] = rest

    def put(r, t, at, vals):
        at += size
        out_ref[r * TILES + t, at : at + 2 * SUB, :] = vals.astype(jnp.bfloat16)

    def done(which, t):
        for r in which:
            send(r * TILES + t, 1)

    far_sums(first_ref, other_ref, second_ref, put, rows, chans, windows, done)
    for copy in copies:
        copy.wait()


def far_packed(got, swap, rows, chans, windows):
    vmem = pl.BlockSpec(memory_space=pltpu.VMEM)
    scratch = [pltpu.VMEM((TILES, rows, chans, 3, windows, LANES), jnp.float32)]
    params = dict(
        compiler_params=pltpu.CompilerParams(vmem_limit_bytes=32 * 2**20),
        cost_estimate=pl.CostEstimate(flops=10**9, bytes_accessed=2**20, transcendentals=0),
    )
    size = 3 * chans * SUB
    sizes = dict(rows=rows, chans=chans, windows=windows)
    first, own = pl.pallas_call(
        functools.partial(far_own_kernel, **sizes),
        out_shape=[
            jax.ShapeDtypeStruct((2, TILES, 3, windows * SUB, LANES), jnp.float32),
            jax.ShapeDtypeStruct((rows * TILES, size, LANES), jnp.bfloat16),
        ],
        in_specs=[vmem],
        out_specs=[vmem] * 2,
        scratch_shapes=scratch,
        name="far_own",
        **params,
    )(got)
    return pl.pallas_call(
        functools.partial(far_other_kernel, **sizes),
        out_shape=jax.ShapeDtypeStruct((rows * TILES, 2 * size, LANES), jnp.bfloat16),
        in_specs=[vmem] * 3,
        out_specs=pl.BlockSpec(memory_space=pltpu.HBM),
        scratch_shapes=scratch
        + [
            pltpu.VMEM((rows * TILES, 2 * size, LANES), jnp.bfloat16),
            pltpu.SemaphoreType.DMA((1 + (rows - 2) * TILES,)),
        ],
        name="far_other",
        **params,
    )(swap(got), first, own)


def halves_kernel(own_ref, keep_ref, give_ref):
    odd = lax.axis_index("row") % 2
    tiles = keep_ref.shape[0]
    keep_ref[...] = own_ref[pl.ds(odd * tiles, tiles)]
    give_ref[...] = own_ref[pl.ds((1 - odd) * tiles, tiles)]


def halves_packed(own):
    vmem = pl.BlockSpec(memory_space=pltpu.VMEM)
    band = jax.ShapeDtypeStruct((own.shape[0] // 2, *own.shape[1:]), own.dtype)
    return pl.pallas_call(
        halves_kernel,
        out_shape=[band] * 2,
        in_specs=[vmem],
        out_specs=[vmem] * 2,
        compiler_params=pltpu.CompilerParams(vmem_limit_bytes=32 * 2**20),
        cost_estimate=pl.CostEstimate(flops=10**9, bytes_accessed=2**20, transcendentals=0),
        name="halves",
    )(own)


def near_kernel(*refs, windows):
    sources, outs, (first_ref, second_ref) = refs[:4], refs[4:6], refs[6:]
    chans = 2
    odd = lax.axis_index("row") % 2
    low = lax.broadcasted_iota(jnp.int32, (SUB, LANES), 0) < SUB // 2
    tiles = outs[0].shape[0]

    def body(m, carry):
        for t in range(TILES):
            tile = m * TILES + t
            first = first_ref.at[t]
            work = []
            for n in range(2):
                own_ref, other_ref = sources[2 * n : 2 * n + 2]
                spread_first(first, odd if n == 0 else 1 - odd, own_ref[tile], windows, chans)
                for s, ref in enumerate((own_ref, other_ref)):
                    spread_second(second_ref.at[t, n, s], ref[tile], windows, chans)
                    work += [(first, second_ref.at[t, n, s, k]) for k in range(chans)]
            sums = pair_sums(work, windows)
            for n, out_ref in enumerate(outs):
                for s in range(2):
                    one, two = sums[(n * 2 + s) * chans : (n * 2 + s + 1) * chans]
                    vals = [
                        jnp.where(low, one[q], pltpu.roll(two[q], SUB // 2, 0)) for q in range(2)
                    ]
                    vals = jnp.concatenate(vals).astype(jnp.bfloat16)
                    out_ref[tile, s * 2 * SUB : (s + 1) * 2 * SUB, :] = vals
        return carry

    lax.fori_loop(0, tiles // TILES, body, 0)


def near_packed(keep, keep_other, took, took_other, windows):
    vmem = pl.BlockSpec(memory_space=pltpu.VMEM)
    piece = jax.ShapeDtypeStruct((keep.shape[0], 4 * SUB, LANES), jnp.bfloat16)
    return pl.pallas_call(
        functools.partial(near_kernel, windows=windows),
        out_shape=[piece] * 2,
        in_specs=[vmem] * 4,
        out_specs=[vmem] * 2,
        scratch_shapes=[
            pltpu.VMEM((TILES, 3, windows * SUB, LANES), jnp.float32),
            pltpu.VMEM((TILES, 2, 2, 2, 3, windows, LANES), jnp.float32),
        ],
        compiler_params=pltpu.CompilerParams(vmem_limit_bytes=32 * 2**20),
        cost_estimate=pl.CostEstimate(flops=10**9, bytes_accessed=2**20, transcendentals=0),
        name="near",
    )(keep, keep_other, took, took_other)


def near_out_kernel(kept_ref, taken_ref, out_hbm, wide_ref, out_ref, sems, *, chans):
    level, odd = lax.axis_index("row") // 2, lax.axis_index("row") % 2
    col = lax.axis_index("col")
    per_row = 2 * chans
    bands, parts, _, quads, _, _ = out_ref.shape
    second = odd * per_row + lax.broadcasted_iota(jnp.int32, (SUB, LANES), 0) % per_row
    for n, ref in enumerate((kept_ref, taken_ref)):
        for m in range(quads):
            for t in range(TILES):
                for s in range(2):
                    side = col if s == 0 else 1 - col
                    vals = ref[m * TILES + t, s * 2 * SUB : (s + 1) * 2 * SUB, :]
                    vals = vals.astype(jnp.float32)
                    for q in range(parts):
                        for k in range(chans):
                            to = (q * SUB + t * per_row + side * chans + k) * SUB
                            part = vals[q * SUB : (q + 1) * SUB]
                            part = part if k == 0 else pltpu.roll(part, SUB // 2, 0)
                            wide_ref[n, m, pl.ds(pl.multiple_of(to, SUB), SUB), :] = part
    copies = []
    for b in range(bands):
        for q in range(parts):
            out_ref[b, q] = jnp.zeros(out_ref.shape[2:], out_ref.dtype)
            for m in range(quads):
                for i in range(per_row):
                    first = i // chans * per_row + col * chans + i % chans
                    spot = pl.ds(q * SUB * SUB + i, SUB, stride=SUB)
                    vals = wide_ref[b ^ odd, m, spot, :]
                    out_ref[b, q, level * per_row + i, m] = jnp.where(first <= second, vals, 0.0)
            sem = sems.at[b * parts + q]
            copies.append(pltpu.make_async_copy(out_ref.at[b, q], out_hbm.at[b, q], sem))
            copies[-1].start()
    for copy in copies:
        copy.wait()


def near_out_packed(kept, taken, rows, chans):
    vmem = pl.BlockSpec(memory_space=pltpu.VMEM)
    shape = (2, 2, rows * chans, rows // 2, SUB, LANES)
    return pl.pallas_call(
        functools.partial(near_out_kernel, chans=chans),
        out_shape=jax.ShapeDtypeStruct(shape, jnp.float32),
        in_specs=[vmem] * 2,
        out_specs=pl.BlockSpec(memory_space=pltpu.HBM),
        scratch_shapes=[
            pltpu.VMEM((2, rows // 2, 2 * SUB * SUB, LANES), jnp.float32),
            pltpu.VMEM(shape, jnp.float32),
            pltpu.SemaphoreType.DMA((4,)),
        ],
        compiler_params=pltpu.CompilerParams(vmem_limit_bytes=32 * 2**20),
        cost_estimate=pl.CostEstimate(flops=10**9, bytes_accessed=2**20, transcendentals=0),
        name="near_out",
    )(kept, taken)


def finish_kernel(far_ref, _, out_hbm, wide_ref, block_ref, sems, *, rows, chans):
    level = lax.axis_index("row") // 2
    col = lax.axis_index("col")
    per_row = 2 * chans
    half = rows // 2
    size = 3 * chans * SUB
    levels, bands, parts = block_ref.shape[:3]

    def widen(piece, of_half, count):
        for r in range(rows):
            for t in range(TILES):
                for s in range(2):
                    side = col if s == 0 else 1 - col
                    vals = far_ref[r * TILES + t, s * size + of_half : s * size + of_half + count, :]
                    vals = vals.astype(jnp.float32)
                    each = count // parts
                    for q in range(parts):
                        for k in range(chans):
                            to = (q * SUB + t * per_row + side * chans + k) * SUB
                            if each == SUB:
                                part = vals[q * SUB : (q + 1) * SUB]
                                part = part if k == 0 else pltpu.roll(part, SUB // 2, 0)
                            else:
                                part = vals[q * each + k * SUB : q * each + (k + 1) * SUB]
                            wide_ref[piece, r, pl.ds(pl.multiple_of(to, SUB), SUB), :] = part

    def copies(z):
        firsts = pl.ds(z * per_row, per_row)
        return [
            pltpu.make_async_copy(
                block_ref.at[z, b, q], out_hbm.at[b, q, firsts], sems.at[z, b * parts + q]
            )
            for b in range(bands)
            for q in range(parts)
        ]

    def send(z):
        piece, at = (z * per_row) // SUB, (z * per_row) % SUB
        for r in range(rows):
            for q in range(parts):
                for i in range(per_row):
                    spot = pl.ds(q * SUB * SUB + at + i, SUB, stride=SUB)
                    block_ref[z, r // half, q, i, r % half] = wide_ref[piece, r, spot, :]
        for copy in copies(z):
            copy.start()

    def wait(z):
        for copy in copies(z):
            copy.wait()

    def first_level():
        widen(0, 0, 2 * chans * SUB)
        send(0)

    def third_level():
        widen(1, 2 * chans * SUB, chans * SUB)
        send(2)

    pl.when(level > 0)(first_level)
    pl.when(level > 1)(lambda: send(1))
    pl.when(level > 2)(third_level)
    for z in range(levels):
        pl.when(level > z)(functools.partial(wait, z))


def finish_packed(far, out, rows, chans):
    hbm = pl.BlockSpec(memory_space=pltpu.HBM)
    levels, quads = rows // 2 - 1, out.shape[3]
    return pl.pallas_call(
        functools.partial(finish_kernel, rows=rows, chans=chans),
        out_shape=jax.ShapeDtypeStruct(out.shape, out.dtype),
        in_specs=[pl.BlockSpec(memory_space=pltpu.VMEM), hbm],
        out_specs=hbm,
        scratch_shapes=[
            pltpu.VMEM((2, rows, 2 * SUB * SUB, LANES), jnp.float32),
            pltpu.VMEM((levels, 2, 2, 2 * chans, quads, SUB, LANES), jnp.float32),
            pltpu.SemaphoreType.DMA((levels, 4)),
        ],
        input_output_aliases={1: 0},
        compiler_params=pltpu.CompilerParams(vmem_limit_bytes=32 * 2**20),
        cost_estimate=pl.CostEstimate(flops=10**9, bytes_accessed=2**20, transcendentals=0),
        name="finish",
    )(far, out)


def on_device_packed(spectra, window_flags):
    bands, windows, parts, chans, bins = spectra.shape
    rows, cols = lax.axis_size("row"), lax.axis_size("col")
    chunks = bins // LANES
    view = spectra.reshape(bands, windows, parts, chans, chunks, LANES)
    view = view.transpose(0, 1, 2, 4, 3, 5).reshape(bands, windows, parts, chunks * chans, LANES)

    def swap(value):
        return lax.ppermute(value, "col", [(0, 1), (1, 0)])

    own = whiten_packed(view, window_flags.T)
    got = lax.all_to_all(own, "row", 0, 0, tiled=True)

    def level_swap(value):
        return lax.ppermute(value, "row", [(r, r ^ 1) for r in range(rows)])

    keep, give = halves_packed(own)
    took = level_swap(give)
    keep_other = swap(keep)
    got, took, keep_other = lax.optimization_barrier((got, took, keep_other))
    far = far_packed(got, swap, rows, chans, windows)
    far = lax.all_to_all(far, "row", 0, 0, tiled=True)
    kept, give = near_packed(keep, keep_other, took, swap(took), windows)
    out = near_out_packed(kept, level_swap(give), rows, chans)
    out = finish_packed(far, out, rows, chans)
    out = out.reshape(bands, 2, rows * chans, chunks, cols * chans, LANES)
    out = out.transpose(0, 1, 2, 4, 3, 5)
    return out.reshape(bands, 2, 1, rows * chans, cols * chans, bins)


def on_device(spectra, window_flags):
    bands, windows, _, chans, bins = spectra.shape
    rows, cols = lax.axis_size("row"), lax.axis_size("col")
    if (
        bands == 2
        and rows == 8
        and bands * bins == rows * TILES * LANES
        and cols == 2
        and chans == 2
        and windows % 32 == 0
        and bins == rows * LANES
    ):
        return on_device_packed(spectra, window_flags)
    payload = whiten_plain(spectra, window_flags, rows * cols)
    got = lax.all_to_all(payload, ("row", "col"), 0, 0, tiled=True)
    result = cross_plain(got, rows, cols, chans, windows)
    back = lax.all_to_all(result, ("row", "col"), 0, 0, tiled=True)
    return finish_plain(back, bands, bins, rows, cols, chans)


def solution(mesh):
    in_specs = (P("parts", None, None, ("row", "col"), None), P("parts", ("row", "col")))
    out_specs = P("parts", None, "col", None, "row", None)
    return jax.shard_map(
        on_device, mesh=mesh, in_specs=in_specs, out_specs=out_specs, check_vma=False
    )
```

```python
import functools

import jax
import jax.numpy as jnp
from jax import lax
from jax.experimental import pallas as pl
from jax.experimental.pallas import tpu as pltpu
from jax.sharding import PartitionSpec as P

HALFWIN = 64
LANES = 128
SUB = 8

epsilon = 1e-06


def window_mean(magnitude):
    bins = magnitude.shape[-1]
    lead = [(0, 0)] * (magnitude.ndim - 1)
    padded = jnp.pad(magnitude, lead + [(HALFWIN + 1, HALFWIN)])
    running = jnp.cumsum(padded, axis=-1)
    total = running[..., 2 * HALFWIN + 1 :] - running[..., :bins]
    positions = jnp.arange(bins, dtype=jnp.int32)
    counted = (
        jnp.minimum(positions + HALFWIN, bins - 1) - jnp.maximum(positions - HALFWIN, 0) + 1
    ).astype(jnp.float32)
    return total / counted


def whiten_plain(spectra, window_flags, devices):
    bands, windows, parts, chans, bins = spectra.shape
    flags = window_flags.astype(jnp.float32)[None, :, None, :, None]
    values = spectra.astype(jnp.float32) * flags
    magnitude = jnp.sqrt(values[:, :, 0] * values[:, :, 0] + values[:, :, 1] * values[:, :, 1])
    smooth = window_mean(magnitude)
    white = (values / (smooth[:, :, None] + epsilon)).astype(jnp.bfloat16)
    own = bands * bins // devices
    white = white.reshape(bands, windows, parts, chans, bins // own, own)
    white = white.transpose(0, 4, 3, 2, 1, 5)
    return white.reshape(devices, chans * parts * windows, own)


def cross_plain(got, rows, cols, chans, windows):
    own = got.shape[-1]
    data = got.reshape(rows * cols * chans, 2, windows, own)
    prods = jnp.einsum("apwf,jqwf->pqajf", data, data, preferred_element_type=jnp.float32)
    both = jnp.stack([prods[0, 0] + prods[1, 1], prods[1, 0] - prods[0, 1]])
    both = both.reshape(2, rows, cols, chans, rows, cols * chans, own)
    both = both.transpose(4, 2, 0, 1, 3, 5, 6).astype(jnp.bfloat16)
    return both.reshape(rows * cols, 2 * rows * chans * cols * chans, own)


def finish_plain(got, bands, bins, rows, cols, chans):
    own = got.shape[-1]
    row, col = lax.axis_index("row"), lax.axis_index("col")
    data = got.reshape(bands, bins // own, 2, rows * chans, cols * chans, own)
    data = data.transpose(0, 2, 3, 4, 1, 5).reshape(
        bands, 2, rows * chans, cols * chans, bins
    )
    slot = jnp.arange(rows * chans, dtype=jnp.int32)
    first = (slot // chans * cols + col) * chans + slot % chans
    second = row * cols * chans + jnp.arange(cols * chans, dtype=jnp.int32)
    keep = (first[:, None] <= second[None, :])[:, :, None]
    return jnp.where(keep, data.astype(jnp.float32), 0.0)[:, :, None]


TILES = 2
VMEM_FIRST = 65454080


def whiten_kernel(
    flags_hbm, x_hbm, out_hbm, flags_ref, x_ref, white_ref, out_ref, sems, out_sems, *, chans
):
    bands, windows, _, group, _ = x_ref.shape
    chunks = group // chans
    step = 32
    steps = windows // step
    rows = step * group

    copies = [pltpu.make_async_copy(flags_hbm, flags_ref, sems.at[bands * steps])]
    for n in range(bands * steps):
        part = (n // steps, pl.ds(n % steps * step, step))
        copies.append(pltpu.make_async_copy(x_hbm.at[part], x_ref.at[part], sems.at[n]))
    for copy in copies:
        copy.start()

    row_id = lax.broadcasted_iota(jnp.int32, (rows, LANES), 0) % group
    lane_id = lax.broadcasted_iota(jnp.int32, (rows, LANES), 1)
    spot = row_id // chans * LANES + lane_id
    last = chunks * LANES - 1
    counted = jnp.minimum(spot + HALFWIN, last) - jnp.maximum(spot - HALFWIN, 0) + 1
    inv_count = 1.0 / counted.astype(jnp.float32)
    has_prev = row_id >= chans
    has_next = row_id < group - chans
    k_id = lax.broadcasted_iota(jnp.int32, (group, LANES), 0) % chans
    src = lax.broadcasted_iota(jnp.int32, (2 * LANES, 3 * LANES), 0) % LANES
    dst = lax.broadcasted_iota(jnp.int32, (2 * LANES, 3 * LANES), 1) - LANES
    band_mat = jnp.where(jnp.abs(src - dst) <= HALFWIN, 1.0, 0.0).astype(jnp.bfloat16)

    for copy in copies:
        copy.wait()
    for b in range(bands):
        for n in range(steps):
            w0 = n * step
            x = x_ref[b, w0 : w0 + step].astype(jnp.float32)
            keeps = []
            for s in range(step):
                keep = jnp.full((group, LANES), flags_ref[0, w0 + s], jnp.int32)
                for k in range(1, chans):
                    keep = jnp.where(k_id == k, flags_ref[k, w0 + s], keep)
                keeps.append(keep)
            keep = jnp.stack(keeps).astype(jnp.float32)
            re = (x[:, 0] * keep).reshape(rows, LANES)
            im = (x[:, 1] * keep).reshape(rows, LANES)
            mag = jnp.sqrt(re * re + im * im)
            high = mag.astype(jnp.bfloat16)
            rest = (mag - high.astype(jnp.float32)).astype(jnp.bfloat16)
            both = jnp.concatenate([high, rest], axis=1)
            sums = jnp.dot(both, band_mat, preferred_element_type=jnp.float32)
            total = sums[:, LANES : 2 * LANES]
            total += jnp.where(has_prev, pltpu.roll(sums[:, 2 * LANES :], chans, 0), 0.0)
            total += jnp.where(has_next, pltpu.roll(sums[:, :LANES], rows - chans, 0), 0.0)
            inv = 1.0 / (total * inv_count + epsilon)
            for p, part in enumerate((re, im)):
                start = ((b * 2 + p) * windows + w0) * group
                white_ref[start : start + rows, :] = part * inv
        for c in range(chunks):
            for k in range(chans):
                for p in range(2):
                    start = (b * 2 + p) * windows * group + c * chans + k
                    slab = white_ref[pl.ds(start, windows, stride=group), :]
                    at = (k * 2 + p) * windows
                    out_ref[b * chunks + c, at : at + windows, :] = slab.astype(jnp.bfloat16)
            if c % TILES == TILES - 1:
                n = (b * chunks + c) // TILES
                part = pl.ds(n * TILES, TILES)
                copy = pltpu.make_async_copy(out_ref.at[part], out_hbm.at[part], out_sems.at[n])
                copy.start()
                copies.append(copy)
    for copy in copies[1 + bands * steps :]:
        copy.wait()


def whiten_packed(view, flags):
    bands, windows, parts, group, _ = view.shape
    chans = flags.shape[0]
    tiles = bands * group // chans
    hbm = pl.BlockSpec(memory_space=pltpu.HBM)
    shape = (tiles, chans * parts * windows, LANES)
    return pl.pallas_call(
        functools.partial(whiten_kernel, chans=chans),
        out_shape=jax.ShapeDtypeStruct(shape, jnp.bfloat16),
        in_specs=[hbm, hbm],
        out_specs=hbm,
        scratch_shapes=[
            pltpu.SMEM(flags.shape, jnp.int32),
            pltpu.VMEM(view.shape, jnp.bfloat16),
            pltpu.VMEM((bands * parts * windows * group, LANES), jnp.float32),
            pltpu.VMEM(shape, jnp.bfloat16),
            pltpu.SemaphoreType.DMA((bands * windows // 32 + 1,)),
            pltpu.SemaphoreType.DMA((tiles // TILES,)),
        ],
        compiler_params=pltpu.CompilerParams(vmem_limit_bytes=VMEM_FIRST),
        cost_estimate=pl.CostEstimate(flops=10**9, bytes_accessed=2**20, transcendentals=0),
        name="whiten",
    )(flags, view)


def spread_second(second_ref, values, windows, chans):
    for k in range(chans):
        row = k * 2 * windows
        re = values[row : row + windows].astype(jnp.float32)
        im = values[row + windows : row + 2 * windows].astype(jnp.float32)
        second_ref[k, 0] = re
        second_ref[k, 1] = im - re
        second_ref[k, 2] = re + im


def spread_first(first_ref, row_at, values, windows, chans):
    for k in range(chans):
        row = k * 2 * windows
        re = values[row : row + windows].astype(jnp.float32)
        im = values[row + windows : row + 2 * windows].astype(jnp.float32)
        slot = pl.ds(row_at * chans + k, windows, stride=SUB)
        first_ref[0, slot, :] = re + im
        first_ref[1, slot, :] = im
        first_ref[2, slot, :] = re


def pair_sums(work, windows):
    zero = jnp.zeros((SUB, LANES), jnp.float32)
    low = lax.broadcasted_iota(jnp.int32, (SUB, LANES), 0) < SUB // 2

    def body(w, sums):
        base = pl.multiple_of(w * SUB, SUB)
        loaded = {}

        def load(ref, at):
            if id(ref) not in loaded:
                loaded[id(ref)] = [ref[q, at, :] for q in range(3)]
            return loaded[id(ref)]

        out = []
        for (first_ref, second_ref), (s1, s2, s3) in zip(work, sums):
            f = load(first_ref, pl.ds(base, SUB))
            if isinstance(second_ref, tuple):
                ends = [load(ref, pl.ds(w, 1)) for ref in second_ref]
                g = [jnp.where(low, one, two) for one, two in zip(*ends)]
            else:
                g = load(second_ref, pl.ds(w, 1))
            out.append((s1 + g[0] * f[0], s2 + g[1] * f[1], s3 + g[2] * f[2]))
        return tuple(out)

    sums = lax.fori_loop(0, windows, body, ((zero, zero, zero),) * len(work), unroll=32)
    return [(s1 + s2, s1 - s3) for s1, s2, s3 in sums]


def far_sums(first_ref, values_ref, second_ref, put, rows, chans, windows, done=None, skip=0):
    for t in range(TILES):
        firsts, last_firsts, level_firsts = (first_ref.at[block, t] for block in range(3))
        seconds = {}
        for r in range(2, rows):
            spread_second(second_ref.at[t, r], values_ref[(r - skip) * TILES + t], windows, chans)
            seconds[r] = tuple(second_ref.at[t, r, k] for k in range(chans))
        mid = range(4, rows - 2)
        work = [(level_firsts, seconds[r]) for r in (2, 3)]
        work += [(firsts, g) for r in mid for g in seconds[r]]
        sums = pair_sums(work, windows)
        for n, r in enumerate((2, 3)):
            for q in range(2):
                vals = sums[n][q]
                vals = jnp.concatenate([vals, pltpu.roll(vals, SUB // 2, 0)])
                put(r, t, q * chans * SUB, vals)
        for n, r in enumerate(mid):
            for q in range(2):
                vals = jnp.concatenate([sums[2 + n * chans + k][q] for k in range(chans)])
                put(r, t, q * chans * SUB, vals)
        if done is not None:
            done(range(2, rows - 2), t)
        last = range(rows - 2, rows)
        work = [(firsts, g) for r in last for g in seconds[r]]
        work += [(last_firsts, seconds[r]) for r in last]
        sums = pair_sums(work, windows)
        for n, r in enumerate(last):
            for q in range(2):
                vals = jnp.concatenate([sums[n * chans + k][q] for k in range(chans)])
                put(r, t, q * chans * SUB, vals)
            rest = sums[len(last) * chans + n]
            put(r, t, 2 * chans * SUB, jnp.concatenate(rest))
        if done is not None:
            done(last, t)


def far_own_kernel(got_ref, first_ref, out_ref, second_ref, *, rows, chans, windows):
    for t in range(TILES):
        for r in range(rows - 2):
            places = [(0, r)] if r < 4 else [(1, r - 4), (1, r - 2)]
            places += [(2, r), (2, r + 2)] if r < 2 else []
            for block, slot in places:
                first = first_ref.at[block, t]
                spread_first(first, slot, got_ref[r * TILES + t], windows, chans)

    def put(r, t, at, vals):
        out_ref[r * TILES + t, at : at + 2 * SUB, :] = vals.astype(jnp.bfloat16)

    far_sums(first_ref, got_ref, second_ref, put, rows, chans, windows)


def far_other_kernel(
    other_ref, first_ref, own_ref, out_hbm, second_ref, out_ref, sems, *, rows, chans, windows
):
    size = own_ref.shape[1]
    copies = []

    def send(first, count):
        part = pl.ds(first, count)
        sem = sems.at[len(copies)]
        copies.append(pltpu.make_async_copy(out_ref.at[part], out_hbm.at[part], sem))
        copies[-1].start()

    out_ref[: 2 * TILES] = jnp.zeros((2 * TILES, *out_ref.shape[1:]), out_ref.dtype)
    send(0, 2 * TILES)
    mid = pl.ds(2 * TILES, (rows - 4) * TILES)
    rest = jnp.zeros(((rows - 4) * TILES, 2 * SUB, LANES), out_ref.dtype)
    out_ref[2 * TILES :, :size, :] = own_ref[2 * TILES :]
    for s in range(2):
        out_ref[mid, s * size + 4 * SUB : s * size + 6 * SUB, :] = rest

    def put(r, t, at, vals):
        at += size
        out_ref[r * TILES + t, at : at + 2 * SUB, :] = vals.astype(jnp.bfloat16)

    def done(which, t):
        for r in which:
            send(r * TILES + t, 1)

    far_sums(first_ref, other_ref, second_ref, put, rows, chans, windows, done, skip=2)
    for copy in copies:
        copy.wait()


def far_packed(got, swap, rows, chans, windows):
    vmem = pl.BlockSpec(memory_space=pltpu.VMEM)
    scratch = [pltpu.VMEM((TILES, rows, chans, 3, windows, LANES), jnp.float32)]
    params = dict(
        compiler_params=pltpu.CompilerParams(vmem_limit_bytes=32 * 2**20),
        cost_estimate=pl.CostEstimate(flops=10**9, bytes_accessed=2**20, transcendentals=0),
    )
    size = 3 * chans * SUB
    sizes = dict(rows=rows, chans=chans, windows=windows)
    first, own = pl.pallas_call(
        functools.partial(far_own_kernel, **sizes),
        out_shape=[
            jax.ShapeDtypeStruct((3, TILES, 3, windows * SUB, LANES), jnp.float32),
            jax.ShapeDtypeStruct((rows * TILES, size, LANES), jnp.bfloat16),
        ],
        in_specs=[vmem],
        out_specs=[vmem] * 2,
        scratch_shapes=scratch,
        name="far_own",
        **params,
    )(got)
    return pl.pallas_call(
        functools.partial(far_other_kernel, **sizes),
        out_shape=jax.ShapeDtypeStruct((rows * TILES, 2 * size, LANES), jnp.bfloat16),
        in_specs=[vmem] * 3,
        out_specs=pl.BlockSpec(memory_space=pltpu.HBM),
        scratch_shapes=scratch
        + [
            pltpu.VMEM((rows * TILES, 2 * size, LANES), jnp.bfloat16),
            pltpu.SemaphoreType.DMA((1 + (rows - 2) * TILES,)),
        ],
        name="far_other",
        **params,
    )(swap(got[2 * TILES :]), first, own)


def halves_kernel(own_ref, keep_ref, give_ref):
    odd = lax.axis_index("row") % 2
    tiles = keep_ref.shape[0]
    keep_ref[...] = own_ref[pl.ds(odd * tiles, tiles)]
    give_ref[...] = own_ref[pl.ds((1 - odd) * tiles, tiles)]


def halves_packed(own):
    vmem = pl.BlockSpec(memory_space=pltpu.VMEM)
    band = jax.ShapeDtypeStruct((own.shape[0] // 2, *own.shape[1:]), own.dtype)
    return pl.pallas_call(
        halves_kernel,
        out_shape=[band] * 2,
        in_specs=[vmem],
        out_specs=[vmem] * 2,
        compiler_params=pltpu.CompilerParams(vmem_limit_bytes=32 * 2**20),
        cost_estimate=pl.CostEstimate(flops=10**9, bytes_accessed=2**20, transcendentals=0),
        name="halves",
    )(own)


def near_kernel(*refs, windows):
    sources, outs, (first_ref, second_ref) = refs[:4], refs[4:6], refs[6:]
    chans = 2
    odd = lax.axis_index("row") % 2
    low = lax.broadcasted_iota(jnp.int32, (SUB, LANES), 0) < SUB // 2
    tiles = outs[0].shape[0]

    def body(m, carry):
        for t in range(TILES):
            tile = m * TILES + t
            first = first_ref.at[t]
            work = []
            for n in range(2):
                own_ref, other_ref = sources[2 * n : 2 * n + 2]
                spread_first(first, odd if n == 0 else 1 - odd, own_ref[tile], windows, chans)
                for s, ref in enumerate((own_ref, other_ref)):
                    spread_second(second_ref.at[t, n, s], ref[tile], windows, chans)
                    work += [(first, second_ref.at[t, n, s, k]) for k in range(chans)]
            sums = pair_sums(work, windows)
            for n, out_ref in enumerate(outs):
                for s in range(2):
                    one, two = sums[(n * 2 + s) * chans : (n * 2 + s + 1) * chans]
                    vals = [
                        jnp.where(low, one[q], pltpu.roll(two[q], SUB // 2, 0)) for q in range(2)
                    ]
                    vals = jnp.concatenate(vals).astype(jnp.bfloat16)
                    out_ref[tile, s * 2 * SUB : (s + 1) * 2 * SUB, :] = vals
        return carry

    lax.fori_loop(0, tiles // TILES, body, 0)


def near_packed(keep, keep_other, took, took_other, windows):
    vmem = pl.BlockSpec(memory_space=pltpu.VMEM)
    piece = jax.ShapeDtypeStruct((keep.shape[0], 4 * SUB, LANES), jnp.bfloat16)
    return pl.pallas_call(
        functools.partial(near_kernel, windows=windows),
        out_shape=[piece] * 2,
        in_specs=[vmem] * 4,
        out_specs=[vmem] * 2,
        scratch_shapes=[
            pltpu.VMEM((TILES, 3, windows * SUB, LANES), jnp.float32),
            pltpu.VMEM((TILES, 2, 2, 2, 3, windows, LANES), jnp.float32),
        ],
        compiler_params=pltpu.CompilerParams(vmem_limit_bytes=32 * 2**20),
        cost_estimate=pl.CostEstimate(flops=10**9, bytes_accessed=2**20, transcendentals=0),
        name="near",
    )(keep, keep_other, took, took_other)


def near_out_kernel(kept_ref, taken_ref, out_hbm, wide_ref, out_ref, sems, *, chans):
    level, odd = lax.axis_index("row") // 2, lax.axis_index("row") % 2
    col = lax.axis_index("col")
    per_row = 2 * chans
    bands, parts, _, quads, _, _ = out_ref.shape
    second = odd * per_row + lax.broadcasted_iota(jnp.int32, (SUB, LANES), 0) % per_row
    for n, ref in enumerate((kept_ref, taken_ref)):
        for m in range(quads):
            for t in range(TILES):
                for s in range(2):
                    side = col if s == 0 else 1 - col
                    vals = ref[m * TILES + t, s * 2 * SUB : (s + 1) * 2 * SUB, :]
                    vals = vals.astype(jnp.float32)
                    for q in range(parts):
                        for k in range(chans):
                            to = (q * SUB + t * per_row + side * chans + k) * SUB
                            part = vals[q * SUB : (q + 1) * SUB]
                            part = part if k == 0 else pltpu.roll(part, SUB // 2, 0)
                            wide_ref[n, m, pl.ds(pl.multiple_of(to, SUB), SUB), :] = part
    copies = []
    for b in range(bands):
        for q in range(parts):
            out_ref[b, q] = jnp.zeros(out_ref.shape[2:], out_ref.dtype)
            for m in range(quads):
                for i in range(per_row):
                    first = i // chans * per_row + col * chans + i % chans
                    spot = pl.ds(q * SUB * SUB + i, SUB, stride=SUB)
                    vals = wide_ref[b ^ odd, m, spot, :]
                    out_ref[b, q, level * per_row + i, m] = jnp.where(first <= second, vals, 0.0)
            sem = sems.at[b * parts + q]
            copies.append(pltpu.make_async_copy(out_ref.at[b, q], out_hbm.at[b, q], sem))
            copies[-1].start()
    for copy in copies:
        copy.wait()


def near_out_packed(kept, taken, rows, chans):
    vmem = pl.BlockSpec(memory_space=pltpu.VMEM)
    shape = (2, 2, rows * chans, rows // 2, SUB, LANES)
    return pl.pallas_call(
        functools.partial(near_out_kernel, chans=chans),
        out_shape=jax.ShapeDtypeStruct(shape, jnp.float32),
        in_specs=[vmem] * 2,
        out_specs=pl.BlockSpec(memory_space=pltpu.HBM),
        scratch_shapes=[
            pltpu.VMEM((2, rows // 2, 2 * SUB * SUB, LANES), jnp.float32),
            pltpu.VMEM(shape, jnp.float32),
            pltpu.SemaphoreType.DMA((4,)),
        ],
        compiler_params=pltpu.CompilerParams(vmem_limit_bytes=32 * 2**20),
        cost_estimate=pl.CostEstimate(flops=10**9, bytes_accessed=2**20, transcendentals=0),
        name="near_out",
    )(kept, taken)


def finish_kernel(far_ref, _, out_hbm, wide_ref, block_ref, sems, *, rows, chans):
    level = lax.axis_index("row") // 2
    col = lax.axis_index("col")
    per_row = 2 * chans
    half = rows // 2
    size = 3 * chans * SUB
    levels, bands, parts = block_ref.shape[:3]

    def widen(piece, of_half, count):
        for r in range(rows):
            for t in range(TILES):
                for s in range(2):
                    side = col if s == 0 else 1 - col
                    vals = far_ref[r * TILES + t, s * size + of_half : s * size + of_half + count, :]
                    vals = vals.astype(jnp.float32)
                    each = count // parts
                    for q in range(parts):
                        for k in range(chans):
                            to = (q * SUB + t * per_row + side * chans + k) * SUB
                            if each == SUB:
                                part = vals[q * SUB : (q + 1) * SUB]
                                part = part if k == 0 else pltpu.roll(part, SUB // 2, 0)
                            else:
                                part = vals[q * each + k * SUB : q * each + (k + 1) * SUB]
                            wide_ref[piece, r, pl.ds(pl.multiple_of(to, SUB), SUB), :] = part

    def copies(z):
        firsts = pl.ds(z * per_row, per_row)
        return [
            pltpu.make_async_copy(
                block_ref.at[z, b, q], out_hbm.at[b, q, firsts], sems.at[z, b * parts + q]
            )
            for b in range(bands)
            for q in range(parts)
        ]

    def send(z):
        piece, at = (z * per_row) // SUB, (z * per_row) % SUB
        for r in range(rows):
            for q in range(parts):
                for i in range(per_row):
                    spot = pl.ds(q * SUB * SUB + at + i, SUB, stride=SUB)
                    block_ref[z, r // half, q, i, r % half] = wide_ref[piece, r, spot, :]
        for copy in copies(z):
            copy.start()

    def wait(z):
        for copy in copies(z):
            copy.wait()

    def first_level():
        widen(0, 0, 2 * chans * SUB)
        send(0)

    def third_level():
        widen(1, 2 * chans * SUB, chans * SUB)
        send(2)

    pl.when(level > 0)(first_level)
    pl.when(level > 1)(lambda: send(1))
    pl.when(level > 2)(third_level)
    for z in range(levels):
        pl.when(level > z)(functools.partial(wait, z))


def finish_packed(far, out, rows, chans):
    hbm = pl.BlockSpec(memory_space=pltpu.HBM)
    levels, quads = rows // 2 - 1, out.shape[3]
    return pl.pallas_call(
        functools.partial(finish_kernel, rows=rows, chans=chans),
        out_shape=jax.ShapeDtypeStruct(out.shape, out.dtype),
        in_specs=[pl.BlockSpec(memory_space=pltpu.VMEM), hbm],
        out_specs=hbm,
        scratch_shapes=[
            pltpu.VMEM((2, rows, 2 * SUB * SUB, LANES), jnp.float32),
            pltpu.VMEM((levels, 2, 2, 2 * chans, quads, SUB, LANES), jnp.float32),
            pltpu.SemaphoreType.DMA((levels, 4)),
        ],
        input_output_aliases={1: 0},
        compiler_params=pltpu.CompilerParams(vmem_limit_bytes=32 * 2**20),
        cost_estimate=pl.CostEstimate(flops=10**9, bytes_accessed=2**20, transcendentals=0),
        name="finish",
    )(far, out)


def on_device_packed(spectra, window_flags):
    bands, windows, parts, chans, bins = spectra.shape
    rows, cols = lax.axis_size("row"), lax.axis_size("col")
    chunks = bins // LANES
    view = spectra.reshape(bands, windows, parts, chans, chunks, LANES)
    view = view.transpose(0, 1, 2, 4, 3, 5).reshape(bands, windows, parts, chunks * chans, LANES)

    def swap(value):
        return lax.ppermute(value, "col", [(0, 1), (1, 0)])

    own = whiten_packed(view, window_flags.T)
    got = lax.all_to_all(own, "row", 0, 0, tiled=True)

    def level_swap(value):
        return lax.ppermute(value, "row", [(r, r ^ 1) for r in range(rows)])

    keep, give = halves_packed(own)
    took = level_swap(give)
    keep_other = swap(keep)
    got, took, keep_other = lax.optimization_barrier((got, took, keep_other))
    far = far_packed(got, swap, rows, chans, windows)
    far = lax.all_to_all(far, "row", 0, 0, tiled=True)
    kept, give = near_packed(keep, keep_other, took, swap(took), windows)
    out = near_out_packed(kept, level_swap(give), rows, chans)
    out = finish_packed(far, out, rows, chans)
    out = out.reshape(bands, 2, rows * chans, chunks, cols * chans, LANES)
    out = out.transpose(0, 1, 2, 4, 3, 5)
    return out.reshape(bands, 2, 1, rows * chans, cols * chans, bins)


def on_device(spectra, window_flags):
    bands, windows, _, chans, bins = spectra.shape
    rows, cols = lax.axis_size("row"), lax.axis_size("col")
    if (
        bands == 2
        and rows == 8
        and bands * bins == rows * TILES * LANES
        and cols == 2
        and chans == 2
        and windows % 32 == 0
        and bins == rows * LANES
    ):
        return on_device_packed(spectra, window_flags)
    payload = whiten_plain(spectra, window_flags, rows * cols)
    got = lax.all_to_all(payload, ("row", "col"), 0, 0, tiled=True)
    result = cross_plain(got, rows, cols, chans, windows)
    back = lax.all_to_all(result, ("row", "col"), 0, 0, tiled=True)
    return finish_plain(back, bands, bins, rows, cols, chans)


def solution(mesh):
    in_specs = (P("parts", None, None, ("row", "col"), None), P("parts", ("row", "col")))
    out_specs = P("parts", None, "col", None, "row", None)
    return jax.shard_map(
        on_device, mesh=mesh, in_specs=in_specs, out_specs=out_specs, check_vma=False
    )
```

```python
import functools

import jax
import jax.numpy as jnp
from jax import lax
from jax.experimental import pallas as pl
from jax.experimental.pallas import tpu as pltpu
from jax.sharding import PartitionSpec as P

HALFWIN = 64
LANES = 128
SUB = 8

epsilon = 1e-06


def window_mean(magnitude):
    bins = magnitude.shape[-1]
    lead = [(0, 0)] * (magnitude.ndim - 1)
    padded = jnp.pad(magnitude, lead + [(HALFWIN + 1, HALFWIN)])
    running = jnp.cumsum(padded, axis=-1)
    total = running[..., 2 * HALFWIN + 1 :] - running[..., :bins]
    positions = jnp.arange(bins, dtype=jnp.int32)
    counted = (
        jnp.minimum(positions + HALFWIN, bins - 1) - jnp.maximum(positions - HALFWIN, 0) + 1
    ).astype(jnp.float32)
    return total / counted


def whiten_plain(spectra, window_flags, devices):
    bands, windows, parts, chans, bins = spectra.shape
    flags = window_flags.astype(jnp.float32)[None, :, None, :, None]
    values = spectra.astype(jnp.float32) * flags
    magnitude = jnp.sqrt(values[:, :, 0] * values[:, :, 0] + values[:, :, 1] * values[:, :, 1])
    smooth = window_mean(magnitude)
    white = (values / (smooth[:, :, None] + epsilon)).astype(jnp.bfloat16)
    own = bands * bins // devices
    white = white.reshape(bands, windows, parts, chans, bins // own, own)
    white = white.transpose(0, 4, 3, 2, 1, 5)
    return white.reshape(devices, chans * parts * windows, own)


def cross_plain(got, rows, cols, chans, windows):
    own = got.shape[-1]
    data = got.reshape(rows * cols * chans, 2, windows, own)
    prods = jnp.einsum("apwf,jqwf->pqajf", data, data, preferred_element_type=jnp.float32)
    both = jnp.stack([prods[0, 0] + prods[1, 1], prods[1, 0] - prods[0, 1]])
    both = both.reshape(2, rows, cols, chans, rows, cols * chans, own)
    both = both.transpose(4, 2, 0, 1, 3, 5, 6).astype(jnp.bfloat16)
    return both.reshape(rows * cols, 2 * rows * chans * cols * chans, own)


def finish_plain(got, bands, bins, rows, cols, chans):
    own = got.shape[-1]
    row, col = lax.axis_index("row"), lax.axis_index("col")
    data = got.reshape(bands, bins // own, 2, rows * chans, cols * chans, own)
    data = data.transpose(0, 2, 3, 4, 1, 5).reshape(
        bands, 2, rows * chans, cols * chans, bins
    )
    slot = jnp.arange(rows * chans, dtype=jnp.int32)
    first = (slot // chans * cols + col) * chans + slot % chans
    second = row * cols * chans + jnp.arange(cols * chans, dtype=jnp.int32)
    keep = (first[:, None] <= second[None, :])[:, :, None]
    return jnp.where(keep, data.astype(jnp.float32), 0.0)[:, :, None]


TILES = 2
VMEM_FIRST = 65454080


def whiten_kernel(
    flags_hbm, x_hbm, out_hbm, flags_ref, x_ref, white_ref, out_ref, sems, out_sems, *, chans
):
    bands, windows, _, group, _ = x_ref.shape
    chunks = group // chans
    step = 32
    steps = windows // step
    rows = step * group

    copies = [pltpu.make_async_copy(flags_hbm, flags_ref, sems.at[bands * steps])]
    for n in range(bands * steps):
        part = (n // steps, pl.ds(n % steps * step, step))
        copies.append(pltpu.make_async_copy(x_hbm.at[part], x_ref.at[part], sems.at[n]))
    for copy in copies:
        copy.start()

    row_id = lax.broadcasted_iota(jnp.int32, (rows, LANES), 0) % group
    lane_id = lax.broadcasted_iota(jnp.int32, (rows, LANES), 1)
    spot = row_id // chans * LANES + lane_id
    last = chunks * LANES - 1
    counted = jnp.minimum(spot + HALFWIN, last) - jnp.maximum(spot - HALFWIN, 0) + 1
    inv_count = 1.0 / counted.astype(jnp.float32)
    has_prev = row_id >= chans
    has_next = row_id < group - chans
    k_id = lax.broadcasted_iota(jnp.int32, (group, LANES), 0) % chans
    src = lax.broadcasted_iota(jnp.int32, (2 * LANES, 3 * LANES), 0) % LANES
    dst = lax.broadcasted_iota(jnp.int32, (2 * LANES, 3 * LANES), 1) - LANES
    band_mat = jnp.where(jnp.abs(src - dst) <= HALFWIN, 1.0, 0.0).astype(jnp.bfloat16)

    for copy in copies:
        copy.wait()
    for b in range(bands):
        for n in range(steps):
            w0 = n * step
            x = x_ref[b, w0 : w0 + step].astype(jnp.float32)
            keeps = []
            for s in range(step):
                keep = jnp.full((group, LANES), flags_ref[0, w0 + s], jnp.int32)
                for k in range(1, chans):
                    keep = jnp.where(k_id == k, flags_ref[k, w0 + s], keep)
                keeps.append(keep)
            keep = jnp.stack(keeps).astype(jnp.float32)
            re = (x[:, 0] * keep).reshape(rows, LANES)
            im = (x[:, 1] * keep).reshape(rows, LANES)
            mag = jnp.sqrt(re * re + im * im)
            high = mag.astype(jnp.bfloat16)
            rest = (mag - high.astype(jnp.float32)).astype(jnp.bfloat16)
            both = jnp.concatenate([high, rest], axis=1)
            sums = jnp.dot(both, band_mat, preferred_element_type=jnp.float32)
            total = sums[:, LANES : 2 * LANES]
            total += jnp.where(has_prev, pltpu.roll(sums[:, 2 * LANES :], chans, 0), 0.0)
            total += jnp.where(has_next, pltpu.roll(sums[:, :LANES], rows - chans, 0), 0.0)
            inv = 1.0 / (total * inv_count + epsilon)
            for p, part in enumerate((re, im)):
                start = ((b * 2 + p) * windows + w0) * group
                white_ref[start : start + rows, :] = part * inv
        for c in range(chunks):
            for k in range(chans):
                for p in range(2):
                    start = (b * 2 + p) * windows * group + c * chans + k
                    slab = white_ref[pl.ds(start, windows, stride=group), :]
                    at = (k * 2 + p) * windows
                    out_ref[b * chunks + c, at : at + windows, :] = slab.astype(jnp.bfloat16)
            if c % TILES == TILES - 1:
                n = (b * chunks + c) // TILES
                part = pl.ds(n * TILES, TILES)
                copy = pltpu.make_async_copy(out_ref.at[part], out_hbm.at[part], out_sems.at[n])
                copy.start()
                copies.append(copy)
    for copy in copies[1 + bands * steps :]:
        copy.wait()


def whiten_packed(view, flags):
    bands, windows, parts, group, _ = view.shape
    chans = flags.shape[0]
    tiles = bands * group // chans
    hbm = pl.BlockSpec(memory_space=pltpu.HBM)
    shape = (tiles, chans * parts * windows, LANES)
    return pl.pallas_call(
        functools.partial(whiten_kernel, chans=chans),
        out_shape=jax.ShapeDtypeStruct(shape, jnp.bfloat16),
        in_specs=[hbm, hbm],
        out_specs=hbm,
        scratch_shapes=[
            pltpu.SMEM(flags.shape, jnp.int32),
            pltpu.VMEM(view.shape, jnp.bfloat16),
            pltpu.VMEM((bands * parts * windows * group, LANES), jnp.float32),
            pltpu.VMEM(shape, jnp.bfloat16),
            pltpu.SemaphoreType.DMA((bands * windows // 32 + 1,)),
            pltpu.SemaphoreType.DMA((tiles // TILES,)),
        ],
        compiler_params=pltpu.CompilerParams(vmem_limit_bytes=VMEM_FIRST),
        cost_estimate=pl.CostEstimate(flops=10**9, bytes_accessed=2**20, transcendentals=0),
        name="whiten",
    )(flags, view)


def spread_second(second_ref, values, windows, chans):
    for k in range(chans):
        row = k * 2 * windows
        re = values[row : row + windows].astype(jnp.float32)
        im = values[row + windows : row + 2 * windows].astype(jnp.float32)
        second_ref[k, 0] = re
        second_ref[k, 1] = im - re
        second_ref[k, 2] = re + im


def spread_first(first_ref, row_at, values, windows, chans):
    for k in range(chans):
        row = k * 2 * windows
        re = values[row : row + windows].astype(jnp.float32)
        im = values[row + windows : row + 2 * windows].astype(jnp.float32)
        slot = pl.ds(row_at * chans + k, windows, stride=SUB)
        first_ref[0, slot, :] = re + im
        first_ref[1, slot, :] = im
        first_ref[2, slot, :] = re


def pair_sums(work, windows):
    zero = jnp.zeros((SUB, LANES), jnp.float32)
    low = lax.broadcasted_iota(jnp.int32, (SUB, LANES), 0) < SUB // 2

    def body(w, sums):
        base = pl.multiple_of(w * SUB, SUB)
        loaded = {}

        def load(ref, at):
            if id(ref) not in loaded:
                loaded[id(ref)] = [ref[q, at, :] for q in range(3)]
            return loaded[id(ref)]

        out = []
        for (first_ref, second_ref), (s1, s2, s3) in zip(work, sums):
            f = load(first_ref, pl.ds(base, SUB))
            if isinstance(second_ref, tuple):
                ends = [load(ref, pl.ds(w, 1)) for ref in second_ref]
                g = [jnp.where(low, one, two) for one, two in zip(*ends)]
            else:
                g = load(second_ref, pl.ds(w, 1))
            out.append((s1 + g[0] * f[0], s2 + g[1] * f[1], s3 + g[2] * f[2]))
        return tuple(out)

    sums = lax.fori_loop(0, windows, body, ((zero, zero, zero),) * len(work), unroll=32)
    return [(s1 + s2, s1 - s3) for s1, s2, s3 in sums]


def far_sums(first_ref, values_ref, second_ref, put, rows, chans, windows, done=None, skip=0):
    tiles = []
    for t in range(TILES):
        firsts, last_firsts, level_firsts = (first_ref.at[block, t] for block in range(3))
        seconds = {}
        for r in range(2, rows):
            spread_second(second_ref.at[t, r], values_ref[(r - skip) * TILES + t], windows, chans)
            seconds[r] = tuple(second_ref.at[t, r, k] for k in range(chans))
        tiles.append((firsts, last_firsts, level_firsts, seconds))
    for t, (firsts, last_firsts, level_firsts, seconds) in enumerate(tiles):
        mid = range(4, rows - 2)
        work = [(level_firsts, seconds[r]) for r in (2, 3)]
        work += [(firsts, g) for r in mid for g in seconds[r]]
        sums = pair_sums(work, windows)
        for n, r in enumerate((2, 3)):
            for q in range(2):
                vals = sums[n][q]
                vals = jnp.concatenate([vals, pltpu.roll(vals, SUB // 2, 0)])
                put(r, t, q * chans * SUB, vals)
        for n, r in enumerate(mid):
            for q in range(2):
                vals = jnp.concatenate([sums[2 + n * chans + k][q] for k in range(chans)])
                put(r, t, q * chans * SUB, vals)
    if done is not None:
        done(range(2, rows - 2))
    for t, (firsts, last_firsts, level_firsts, seconds) in enumerate(tiles):
        last = range(rows - 2, rows)
        work = [(firsts, g) for r in last for g in seconds[r]]
        work += [(last_firsts, seconds[r]) for r in last]
        sums = pair_sums(work, windows)
        for n, r in enumerate(last):
            for q in range(2):
                vals = jnp.concatenate([sums[n * chans + k][q] for k in range(chans)])
                put(r, t, q * chans * SUB, vals)
            rest = sums[len(last) * chans + n]
            put(r, t, 2 * chans * SUB, jnp.concatenate(rest))
    if done is not None:
        done(range(rows - 2, rows))


def far_own_kernel(got_ref, first_ref, out_ref, second_ref, *, rows, chans, windows):
    for t in range(TILES):
        for r in range(rows - 2):
            places = [(0, r)] if r < 4 else [(1, r - 4), (1, r - 2)]
            places += [(2, r), (2, r + 2)] if r < 2 else []
            for block, slot in places:
                first = first_ref.at[block, t]
                spread_first(first, slot, got_ref[r * TILES + t], windows, chans)

    def put(r, t, at, vals):
        out_ref[r * TILES + t, at : at + 2 * SUB, :] = vals.astype(jnp.bfloat16)

    far_sums(first_ref, got_ref, second_ref, put, rows, chans, windows)


def far_other_kernel(
    other_ref, first_ref, own_ref, out_hbm, second_ref, out_ref, sems, *, rows, chans, windows
):
    size = own_ref.shape[1]
    copies = []

    def send(first, count):
        part = pl.ds(first, count)
        sem = sems.at[len(copies)]
        copies.append(pltpu.make_async_copy(out_ref.at[part], out_hbm.at[part], sem))
        copies[-1].start()

    out_ref[: 2 * TILES] = jnp.zeros((2 * TILES, *out_ref.shape[1:]), out_ref.dtype)
    send(0, 2 * TILES)
    mid = pl.ds(2 * TILES, (rows - 4) * TILES)
    rest = jnp.zeros(((rows - 4) * TILES, 2 * SUB, LANES), out_ref.dtype)
    out_ref[2 * TILES :, :size, :] = own_ref[2 * TILES :]
    for s in range(2):
        out_ref[mid, s * size + 4 * SUB : s * size + 6 * SUB, :] = rest

    def put(r, t, at, vals):
        at += size
        out_ref[r * TILES + t, at : at + 2 * SUB, :] = vals.astype(jnp.bfloat16)

    def done(which):
        for r in which:
            send(r * TILES, TILES)

    far_sums(first_ref, other_ref, second_ref, put, rows, chans, windows, done, skip=2)
    for copy in copies:
        copy.wait()


def far_packed(got, swap, rows, chans, windows):
    vmem = pl.BlockSpec(memory_space=pltpu.VMEM)
    scratch = [pltpu.VMEM((TILES, rows, chans, 3, windows, LANES), jnp.float32)]
    params = dict(
        compiler_params=pltpu.CompilerParams(vmem_limit_bytes=32 * 2**20),
        cost_estimate=pl.CostEstimate(flops=10**9, bytes_accessed=2**20, transcendentals=0),
    )
    size = 3 * chans * SUB
    sizes = dict(rows=rows, chans=chans, windows=windows)
    first, own = pl.pallas_call(
        functools.partial(far_own_kernel, **sizes),
        out_shape=[
            jax.ShapeDtypeStruct((3, TILES, 3, windows * SUB, LANES), jnp.float32),
            jax.ShapeDtypeStruct((rows * TILES, size, LANES), jnp.bfloat16),
        ],
        in_specs=[vmem],
        out_specs=[vmem] * 2,
        scratch_shapes=scratch,
        name="far_own",
        **params,
    )(got)
    return pl.pallas_call(
        functools.partial(far_other_kernel, **sizes),
        out_shape=jax.ShapeDtypeStruct((rows * TILES, 2 * size, LANES), jnp.bfloat16),
        in_specs=[vmem] * 3,
        out_specs=pl.BlockSpec(memory_space=pltpu.HBM),
        scratch_shapes=scratch
        + [
            pltpu.VMEM((rows * TILES, 2 * size, LANES), jnp.bfloat16),
            pltpu.SemaphoreType.DMA((rows - 1,)),
        ],
        name="far_other",
        **params,
    )(swap(got[2 * TILES :]), first, own)


def halves_kernel(own_ref, keep_ref, give_ref):
    odd = lax.axis_index("row") % 2
    tiles = keep_ref.shape[0]
    keep_ref[...] = own_ref[pl.ds(odd * tiles, tiles)]
    give_ref[...] = own_ref[pl.ds((1 - odd) * tiles, tiles)]


def halves_packed(own):
    vmem = pl.BlockSpec(memory_space=pltpu.VMEM)
    band = jax.ShapeDtypeStruct((own.shape[0] // 2, *own.shape[1:]), own.dtype)
    return pl.pallas_call(
        halves_kernel,
        out_shape=[band] * 2,
        in_specs=[vmem],
        out_specs=[vmem] * 2,
        compiler_params=pltpu.CompilerParams(vmem_limit_bytes=32 * 2**20),
        cost_estimate=pl.CostEstimate(flops=10**9, bytes_accessed=2**20, transcendentals=0),
        name="halves",
    )(own)


def near_kernel(*refs, windows):
    sources, outs, (first_ref, second_ref) = refs[:4], refs[4:6], refs[6:]
    chans = 2
    odd = lax.axis_index("row") % 2
    low = lax.broadcasted_iota(jnp.int32, (SUB, LANES), 0) < SUB // 2
    tiles = outs[0].shape[0]

    def body(m, carry):
        for t in range(TILES):
            tile = m * TILES + t
            first = first_ref.at[t]
            work = []
            for n in range(2):
                own_ref, other_ref = sources[2 * n : 2 * n + 2]
                spread_first(first, odd if n == 0 else 1 - odd, own_ref[tile], windows, chans)
                for s, ref in enumerate((own_ref, other_ref)):
                    spread_second(second_ref.at[t, n, s], ref[tile], windows, chans)
                    work += [(first, second_ref.at[t, n, s, k]) for k in range(chans)]
            sums = pair_sums(work, windows)
            for n, out_ref in enumerate(outs):
                for s in range(2):
                    one, two = sums[(n * 2 + s) * chans : (n * 2 + s + 1) * chans]
                    vals = [
                        jnp.where(low, one[q], pltpu.roll(two[q], SUB // 2, 0)) for q in range(2)
                    ]
                    vals = jnp.concatenate(vals).astype(jnp.bfloat16)
                    out_ref[tile, s * 2 * SUB : (s + 1) * 2 * SUB, :] = vals
        return carry

    lax.fori_loop(0, tiles // TILES, body, 0)


def near_packed(keep, keep_other, took, took_other, windows):
    vmem = pl.BlockSpec(memory_space=pltpu.VMEM)
    piece = jax.ShapeDtypeStruct((keep.shape[0], 4 * SUB, LANES), jnp.bfloat16)
    return pl.pallas_call(
        functools.partial(near_kernel, windows=windows),
        out_shape=[piece] * 2,
        in_specs=[vmem] * 4,
        out_specs=[vmem] * 2,
        scratch_shapes=[
            pltpu.VMEM((TILES, 3, windows * SUB, LANES), jnp.float32),
            pltpu.VMEM((TILES, 2, 2, 2, 3, windows, LANES), jnp.float32),
        ],
        compiler_params=pltpu.CompilerParams(vmem_limit_bytes=32 * 2**20),
        cost_estimate=pl.CostEstimate(flops=10**9, bytes_accessed=2**20, transcendentals=0),
        name="near",
    )(keep, keep_other, took, took_other)


def near_out_kernel(kept_ref, taken_ref, out_hbm, wide_ref, out_ref, sems, *, chans):
    level, odd = lax.axis_index("row") // 2, lax.axis_index("row") % 2
    col = lax.axis_index("col")
    per_row = 2 * chans
    bands, parts, _, quads, _, _ = out_ref.shape
    second = odd * per_row + lax.broadcasted_iota(jnp.int32, (SUB, LANES), 0) % per_row
    for n, ref in enumerate((kept_ref, taken_ref)):
        for m in range(quads):
            for t in range(TILES):
                for s in range(2):
                    side = col if s == 0 else 1 - col
                    vals = ref[m * TILES + t, s * 2 * SUB : (s + 1) * 2 * SUB, :]
                    vals = vals.astype(jnp.float32)
                    for q in range(parts):
                        for k in range(chans):
                            to = (q * SUB + t * per_row + side * chans + k) * SUB
                            part = vals[q * SUB : (q + 1) * SUB]
                            part = part if k == 0 else pltpu.roll(part, SUB // 2, 0)
                            wide_ref[n, m, pl.ds(pl.multiple_of(to, SUB), SUB), :] = part
    copies = []
    for b in range(bands):
        for q in range(parts):
            out_ref[b, q] = jnp.zeros(out_ref.shape[2:], out_ref.dtype)
            for m in range(quads):
                for i in range(per_row):
                    first = i // chans * per_row + col * chans + i % chans
                    spot = pl.ds(q * SUB * SUB + i, SUB, stride=SUB)
                    vals = wide_ref[b ^ odd, m, spot, :]
                    out_ref[b, q, level * per_row + i, m] = jnp.where(first <= second, vals, 0.0)
            sem = sems.at[b * parts + q]
            copies.append(pltpu.make_async_copy(out_ref.at[b, q], out_hbm.at[b, q], sem))
            copies[-1].start()
    for copy in copies:
        copy.wait()


def near_out_packed(kept, taken, rows, chans):
    vmem = pl.BlockSpec(memory_space=pltpu.VMEM)
    shape = (2, 2, rows * chans, rows // 2, SUB, LANES)
    return pl.pallas_call(
        functools.partial(near_out_kernel, chans=chans),
        out_shape=jax.ShapeDtypeStruct(shape, jnp.float32),
        in_specs=[vmem] * 2,
        out_specs=pl.BlockSpec(memory_space=pltpu.HBM),
        scratch_shapes=[
            pltpu.VMEM((2, rows // 2, 2 * SUB * SUB, LANES), jnp.float32),
            pltpu.VMEM(shape, jnp.float32),
            pltpu.SemaphoreType.DMA((4,)),
        ],
        compiler_params=pltpu.CompilerParams(vmem_limit_bytes=32 * 2**20),
        cost_estimate=pl.CostEstimate(flops=10**9, bytes_accessed=2**20, transcendentals=0),
        name="near_out",
    )(kept, taken)


def finish_kernel(far_ref, _, out_hbm, wide_ref, block_ref, sems, *, rows, chans):
    level = lax.axis_index("row") // 2
    col = lax.axis_index("col")
    per_row = 2 * chans
    half = rows // 2
    size = 3 * chans * SUB
    levels, bands, parts = block_ref.shape[:3]

    def widen(piece, of_half, count):
        for r in range(rows):
            for t in range(TILES):
                for s in range(2):
                    side = col if s == 0 else 1 - col
                    vals = far_ref[r * TILES + t, s * size + of_half : s * size + of_half + count, :]
                    vals = vals.astype(jnp.float32)
                    each = count // parts
                    for q in range(parts):
                        for k in range(chans):
                            to = (q * SUB + t * per_row + side * chans + k) * SUB
                            if each == SUB:
                                part = vals[q * SUB : (q + 1) * SUB]
                                part = part if k == 0 else pltpu.roll(part, SUB // 2, 0)
                            else:
                                part = vals[q * each + k * SUB : q * each + (k + 1) * SUB]
                            wide_ref[piece, r, pl.ds(pl.multiple_of(to, SUB), SUB), :] = part

    def copies(z):
        firsts = pl.ds(z * per_row, per_row)
        return [
            pltpu.make_async_copy(
                block_ref.at[z, b, q], out_hbm.at[b, q, firsts], sems.at[z, b * parts + q]
            )
            for b in range(bands)
            for q in range(parts)
        ]

    def send(z):
        piece, at = (z * per_row) // SUB, (z * per_row) % SUB
        for r in range(rows):
            for q in range(parts):
                for i in range(per_row):
                    spot = pl.ds(q * SUB * SUB + at + i, SUB, stride=SUB)
                    block_ref[z, r // half, q, i, r % half] = wide_ref[piece, r, spot, :]
        for copy in copies(z):
            copy.start()

    def wait(z):
        for copy in copies(z):
            copy.wait()

    def first_level():
        widen(0, 0, 2 * chans * SUB)
        send(0)

    def third_level():
        widen(1, 2 * chans * SUB, chans * SUB)
        send(2)

    pl.when(level > 0)(first_level)
    pl.when(level > 1)(lambda: send(1))
    pl.when(level > 2)(third_level)
    for z in range(levels):
        pl.when(level > z)(functools.partial(wait, z))


def finish_packed(far, out, rows, chans):
    hbm = pl.BlockSpec(memory_space=pltpu.HBM)
    levels, quads = rows // 2 - 1, out.shape[3]
    return pl.pallas_call(
        functools.partial(finish_kernel, rows=rows, chans=chans),
        out_shape=jax.ShapeDtypeStruct(out.shape, out.dtype),
        in_specs=[pl.BlockSpec(memory_space=pltpu.VMEM), hbm],
        out_specs=hbm,
        scratch_shapes=[
            pltpu.VMEM((2, rows, 2 * SUB * SUB, LANES), jnp.float32),
            pltpu.VMEM((levels, 2, 2, 2 * chans, quads, SUB, LANES), jnp.float32),
            pltpu.SemaphoreType.DMA((levels, 4)),
        ],
        input_output_aliases={1: 0},
        compiler_params=pltpu.CompilerParams(vmem_limit_bytes=32 * 2**20),
        cost_estimate=pl.CostEstimate(flops=10**9, bytes_accessed=2**20, transcendentals=0),
        name="finish",
    )(far, out)


def on_device_packed(spectra, window_flags):
    bands, windows, parts, chans, bins = spectra.shape
    rows, cols = lax.axis_size("row"), lax.axis_size("col")
    chunks = bins // LANES
    view = spectra.reshape(bands, windows, parts, chans, chunks, LANES)
    view = view.transpose(0, 1, 2, 4, 3, 5).reshape(bands, windows, parts, chunks * chans, LANES)

    def swap(value):
        return lax.ppermute(value, "col", [(0, 1), (1, 0)])

    own = whiten_packed(view, window_flags.T)
    got = lax.all_to_all(own, "row", 0, 0, tiled=True)

    def level_swap(value):
        return lax.ppermute(value, "row", [(r, r ^ 1) for r in range(rows)])

    keep, give = halves_packed(own)
    took = level_swap(give)
    keep_other = swap(keep)
    got, took, keep_other = lax.optimization_barrier((got, took, keep_other))
    far = far_packed(got, swap, rows, chans, windows)
    far = lax.all_to_all(far, "row", 0, 0, tiled=True)
    kept, give = near_packed(keep, keep_other, took, swap(took), windows)
    out = near_out_packed(kept, level_swap(give), rows, chans)
    out = finish_packed(far, out, rows, chans)
    out = out.reshape(bands, 2, rows * chans, chunks, cols * chans, LANES)
    out = out.transpose(0, 1, 2, 4, 3, 5)
    return out.reshape(bands, 2, 1, rows * chans, cols * chans, bins)


def on_device(spectra, window_flags):
    bands, windows, _, chans, bins = spectra.shape
    rows, cols = lax.axis_size("row"), lax.axis_size("col")
    if (
        bands == 2
        and rows == 8
        and bands * bins == rows * TILES * LANES
        and cols == 2
        and chans == 2
        and windows % 32 == 0
        and bins == rows * LANES
    ):
        return on_device_packed(spectra, window_flags)
    payload = whiten_plain(spectra, window_flags, rows * cols)
    got = lax.all_to_all(payload, ("row", "col"), 0, 0, tiled=True)
    result = cross_plain(got, rows, cols, chans, windows)
    back = lax.all_to_all(result, ("row", "col"), 0, 0, tiled=True)
    return finish_plain(back, bands, bins, rows, cols, chans)


def solution(mesh):
    in_specs = (P("parts", None, None, ("row", "col"), None), P("parts", ("row", "col")))
    out_specs = P("parts", None, "col", None, "row", None)
    return jax.shard_map(
        on_device, mesh=mesh, in_specs=in_specs, out_specs=out_specs, check_vma=False
    )
```
